768 devices in a mesh: grp: 12 (over x, z_hi), col: 64 (over z_lo, y, core).
Axes of the slice: x: 4, y: 8, z: 12 (z_hi: 3, z_lo: 4; z = z_hi * 4 + z_lo), core: 2. Of those that a mesh axis runs over, the one named last changes fastest.
Arguments:
- projected: bfloat16 [64, 1728, 3072], P('col', 'grp'), may hold values from -6 to 6
- out_grad: bfloat16 [64, 1728, 512], P('col', 'grp'), may hold values from -6 to 6
- w_out: bfloat16 [768, 512], replicated, may hold values from -0.21875 to 0.21875
- owners: int32 [64, 144], P('col', 'grp'), may hold values from 0 to 11, as said below
- slots: int32 [64, 144], P('col', 'grp'), may hold values from 0 to 11, as said below
- lengths: int32 [64, 144], P('col', 'grp'), may hold values from 0 to 144, as said below
Outputs:
- branch_out: bfloat16 [64, 1728, 512], P('col', 'grp')
- projected_grad: bfloat16 [64, 1728, 3072], P('col', 'grp')
- output_weight_grad: float32 [768, 512], P('grp', 'col')
The draws below stay inside these ranges and needn't reach their ends.
Inputs may be any that keep to these rules, and one draw needn't show every extreme that they name: In every group, the 12 blocks of each grp index have 12 different owners. In every group, the blocks sent to one owner take each of its 12 slots once. `lengths`: in every group, slot 0 of each owner starts a history; a history that covers k slots has a length over 12 * (k - 1) and at most 12 * k; in every group one owner holds a single history of 144 rows.
All inputs are finite; a program needn't handle non-finite values.
Results may differ from the reference program's by a relative error of at most 0.0063.
Values may be sent and summed in bfloat16 or wider, within the bound.
A program may use at most 128 MiB of HBM per device.

```python
import math
import jax
import jax.numpy as jnp
from jax import lax

D = 512
DH = 128
BR = 12
HD = 768
NB = 12
ROWS_G = 1728
N_GRP = 12
N_COL = 64


def history_tables(key):
    key_sources, key_owners, key_cuts, key_tails, key_full = jax.random.split(key, 5)
    groups = N_COL
    count = N_GRP
    source_keys = jax.random.split(key_sources, groups * count)
    sources = jax.vmap(lambda one: jax.random.permutation(one, count))(source_keys).reshape(groups, count, count)
    slot_of = jnp.argsort(sources, axis=2).astype(jnp.int32)
    owner_keys = jax.random.split(key_owners, groups * count)
    owner_of = jax.vmap(lambda one: jax.random.permutation(one, count))(owner_keys).reshape(groups, count, count).astype(jnp.int32)
    slot_table = jnp.transpose(slot_of, (0, 2, 1))
    slot_drawn = jnp.take_along_axis(slot_table, owner_of, axis=2).astype(jnp.int32)
    places = jnp.arange(count, dtype=jnp.int32)
    full = jax.random.randint(key_full, (groups, 1, 1), 0, count)
    owner_index = places[None, :, None]
    slot_index = places[None, None, :]
    cuts = jax.random.randint(key_cuts, (groups, count, count), 0, 2)
    cuts = jnp.where(owner_index == full, 0, cuts)
    cuts = jnp.where(slot_index == 0, 1, cuts).astype(jnp.int32)
    segment = (jnp.cumsum(cuts, axis=2) - 1).astype(jnp.int32)
    span = jnp.sum((segment[:, :, :, None] == segment[:, :, None, :]).astype(jnp.int32), axis=3).astype(jnp.int32)
    tails = jax.random.randint(key_tails, (groups, count, count), 1, BR + 1)
    tails = jnp.where(owner_index == full, BR, tails)
    length = jnp.where(cuts == 1, BR * (span - 1) + tails, 0).astype(jnp.int32)
    return (owner_of.reshape(groups, count * count), slot_drawn.reshape(groups, count * count), length.reshape(groups, count * count))


def draw_owners(key, part):
    return history_tables(key)[0]


def draw_slots(key, part):
    return history_tables(key)[1]


def draw_lengths(key, part):
    return history_tables(key)[2]


def block_scale(stream_key, extent, cuts, low, largest):
    level = 1.0
    for dim, parts in cuts:
        heights = jax.random.uniform(jax.random.fold_in(jax.random.fold_in(stream_key, 6), dim), (parts,), jnp.float32, low / len(cuts), largest / len(cuts))
        level = level * jnp.repeat(jnp.exp(heights), extent[dim] // parts).reshape((-1,) + (1,) * (len(extent) - 1 - dim))
    return level


def bell_draw(key, extent, scale, limit, cuts=(), held_as=jnp.bfloat16):
    result = scale * jax.random.normal(key, extent, jnp.float32)
    if cuts:
        result = result * block_scale(key, extent, cuts, -0.22, 0.18)
    return jnp.clip(result, -limit, limit).astype(held_as)


def setup_inputs(seed: int = 0) -> dict:
    key_list = jax.random.split(jax.random.key(seed), 7)
    return {
        "projected": bell_draw(key_list[0], (N_COL, ROWS_G, 4 * HD), 1.0, 6.0, ((0, 64), (1, 12))),
        "out_grad": bell_draw(key_list[1], (N_COL, ROWS_G, D), 1.0, 6.0, ((0, 64), (1, 12))),
        "w_out": bell_draw(key_list[2], (HD, D), HD ** -0.5, 0.21875),
        "owners": draw_owners(jax.random.fold_in(key_list[6], 71), 0),
        "slots": draw_slots(jax.random.fold_in(key_list[6], 71), 0),
        "lengths": draw_lengths(jax.random.fold_in(key_list[6], 71), 0),
    }


def history_layout(starts, block_rows):
    count = starts.shape[0]
    opened = (starts > 0).astype(jnp.int32)
    segment = (jnp.cumsum(opened) - 1).astype(jnp.int32)
    places = jnp.arange(count, dtype=jnp.int32)
    shared = segment[:, None] == segment[None, :]
    first = lax.optimization_barrier(jnp.min(jnp.where(shared, places[None, :], count), axis=1)).astype(jnp.int32)
    length = lax.optimization_barrier(jnp.sum(jnp.where(places[None, :] == first[:, None], starts[None, :], 0), axis=1)).astype(jnp.int32)
    inner = jnp.arange(count * block_rows, dtype=jnp.int32)
    block_of = inner // block_rows
    row_segment = jnp.repeat(segment, block_rows)
    position = (block_of - jnp.repeat(first, block_rows)) * block_rows + inner % block_rows
    row_length = jnp.repeat(length, block_rows)
    valid = position < row_length
    mask = (row_segment[:, None] == row_segment[None, :]) & (inner[None, :] <= inner[:, None]) & valid[:, None]
    return (mask, valid, row_length)

def score_product(form, left, right):
    return jnp.einsum(form, left.astype(jnp.float32), right.astype(jnp.float32))

def owner_step(stacked, branch, starts, block_rows):
    mask, valid, row_length = history_layout(starts, block_rows)
    row_counts_total, width = stacked.shape
    feature_rows = width // 4
    heads = feature_rows // DH
    gate = stacked[:, :feature_rows].astype(jnp.float32)
    value_rows = stacked[:, feature_rows:2 * feature_rows].reshape(row_counts_total, heads, DH)
    query_rows = stacked[:, 2 * feature_rows:3 * feature_rows].reshape(row_counts_total, heads, DH)
    key_rows = stacked[:, 3 * feature_rows:].reshape(row_counts_total, heads, DH)
    score_scale = 1.0 / math.sqrt(DH)
    score_matrix = score_product('uej,kej->euk', query_rows, key_rows) * score_scale
    inverse = (1.0 / row_length.astype(jnp.float32))[None, :, None]
    weights = jnp.where(mask[None], jax.nn.silu(score_matrix), 0.0) * inverse
    weights_reduced_precision = weights.astype(jnp.bfloat16)
    attended_output = score_product('xry,yxk->rxk', weights_reduced_precision, value_rows).reshape(row_counts_total, feature_rows)
    centre = lax.optimization_barrier(jnp.mean(attended_output, axis=-1, keepdims=True))
    spread = lax.optimization_barrier(jnp.mean((attended_output - centre) ** 2, axis=-1, keepdims=True))
    rstd = lax.rsqrt(spread + 1e-05)
    normed = (attended_output - centre) * rstd
    mixed = (normed * gate).astype(jnp.bfloat16)
    upstream = branch.astype(jnp.float32)
    gate_grad = (upstream * normed).astype(jnp.bfloat16)
    normed_grad = upstream * gate
    attended_output_grad = rstd * (normed_grad - lax.optimization_barrier(jnp.mean(normed_grad, axis=-1, keepdims=True)) - normed * lax.optimization_barrier(jnp.mean(normed_grad * normed, axis=-1, keepdims=True)))
    attended_output_grad = jnp.where(valid[:, None], attended_output_grad, 0.0).astype(jnp.bfloat16).reshape(row_counts_total, heads, DH)
    output_weight_grad = score_product('uej,kej->euk', attended_output_grad, value_rows)
    value_rows_grad = score_product('ove,vox->eox', weights_reduced_precision, attended_output_grad).astype(jnp.bfloat16)
    sigma = jax.nn.sigmoid(score_matrix)
    scores_gradient = (jnp.where(mask[None], output_weight_grad * sigma * (1.0 + score_matrix * (1.0 - sigma)), 0.0) * inverse).astype(jnp.bfloat16)
    query_rows_grad = (score_product('xry,yxk->rxk', scores_gradient, key_rows) * score_scale).astype(jnp.bfloat16)
    key_rows_grad = (score_product('ove,vox->eox', scores_gradient, query_rows) * score_scale).astype(jnp.bfloat16)
    grads = jnp.concatenate([gate_grad, value_rows_grad.reshape(row_counts_total, feature_rows), query_rows_grad.reshape(row_counts_total, feature_rows), key_rows_grad.reshape(row_counts_total, feature_rows)], axis=-1)
    return (grads, mixed)

def reference(projected, out_grad, w_out, owners, slots, lengths):
    groups = N_GRP
    blocks_dev = NB
    block_rows = BR
    width = projected.shape[-1]

    def group(total, items):
        stacked, upstream, owner_row, slot_row, start_row = items
        branch = jnp.dot(upstream, w_out.T, preferred_element_type=jnp.float32).astype(jnp.bfloat16)
        blocks = stacked.reshape(groups * blocks_dev, block_rows, width)
        branch_blocks = branch.reshape(groups * blocks_dev, block_rows, HD)
        held = jnp.zeros((groups, blocks_dev, block_rows, width), jnp.bfloat16).at[owner_row, slot_row].set(blocks)
        held_branch = jnp.zeros((groups, blocks_dev, block_rows, HD), jnp.bfloat16).at[owner_row, slot_row].set(branch_blocks)

        def one_owner(rows_in, branch_in, starts):
            return owner_step(rows_in.reshape(blocks_dev * block_rows, width), branch_in.reshape(blocks_dev * block_rows, HD), starts, block_rows)
        grads, mixed = jax.vmap(one_owner)(held, held_branch, start_row.reshape(groups, blocks_dev))
        grads = grads.reshape(groups, blocks_dev, block_rows, width)[owner_row, slot_row].reshape(ROWS_G, width)
        mixed = mixed.reshape(groups, blocks_dev, block_rows, HD)[owner_row, slot_row].reshape(ROWS_G, HD)
        output = jnp.dot(mixed, w_out, preferred_element_type=jnp.float32).astype(jnp.bfloat16)
        total = total + jnp.dot(mixed.T, upstream, preferred_element_type=jnp.float32)
        return (total, (output, grads))
    total, (output, grads) = lax.scan(group, jnp.zeros((HD, D), jnp.float32), (projected, out_grad, owners, slots, lengths))
    return (output, grads, total)
```

```python
import functools
import math

import jax
import jax.numpy as jnp
from jax import lax
from jax.experimental import pallas as pl
from jax.experimental.pallas import tpu as pltpu
from jax.sharding import PartitionSpec as P

DH = 128
HEADS = 6
HD = 768
BR = 12
PR = 16
NG = 12
NZ, NY, NC = 4, 8, 2
ROWS = BR * NG
PROWS = PR * NG
MESH = pl.DeviceIdType.MESH
BF = jnp.bfloat16
F32 = jnp.float32


def mm(a, b):
    return lax.dot_general(a, b, (((1,), (0,)), ((), ())), preferred_element_type=F32)


def mm_nt(a, b):
    return lax.dot_general(a, b, (((1,), (1,)), ((), ())), preferred_element_type=F32)


def mm_tn(a, b):
    return lax.dot_general(a, b, (((0,), (0,)), ((), ())), preferred_element_type=F32)


def onehot(cond):
    return jnp.where(cond, 1.0, 0.0).astype(BF)


def iota(shape, dim):
    return lax.broadcasted_iota(jnp.int32, shape, dim)


def fold_in(mats, natural, pair):
    parts = [mm(mats[b], pair) for b in range(3)]
    extra = jnp.concatenate([p[:, :DH] for p in parts] + [p[:, DH:] for p in parts], axis=1)
    return (natural + extra).astype(BF)


def fold_out(mats, chunk):
    total = None
    for b in range(3):
        pair = jnp.concatenate(
            [chunk[:, b * DH : (b + 1) * DH], chunk[:, (3 + b) * DH : (4 + b) * DH]], axis=1
        )
        term = mm(mats[b], pair)
        total = term if total is None else total + term
    return total


def head(h):
    return slice(h * DH, (h + 1) * DH)


def kernel(
    own_s, slot_s, len_s, x_ref, og_ref, w_ref,
    bo_ref, pg_ref, dw_ref,
    cs, cr, rs, rr, ts, tr, p_scr, f_scr, dwf, d1s, d1r, d2s, d2r, d3s, d3r, d4s, d4r,
    c_ssem, c_rsem, r_ssem, r_rsem, t_ssem, t_rsem,
    d1_ssem, d1_rsem, d2_ssem, d2_rsem, d3_ssem, d3_rsem, d4_ssem, d4_rsem,
):
    g = lax.axis_index("grp")
    col = lax.axis_index("col")
    core = lax.rem(col, NC)
    y = lax.rem(col // NC, NY)
    zl = col // (NC * NY)

    def col_of(z_, y_, c_):
        return (z_ * NY + y_) * NC + c_

    other = col_of(zl, y, 1 - core)

    barrier = pltpu.get_barrier_semaphore()

    def greet(k, c):
        pl.semaphore_signal(
            barrier, inc=1, device_id=(lax.rem(g + k, NG), col), device_id_type=MESH
        )
        return c

    lax.fori_loop(1, NG, greet, 0)
    pl.semaphore_signal(barrier, inc=1, device_id=(g, other), device_id_type=MESH)

    def greet_y(k, c):
        pl.semaphore_signal(
            barrier, inc=1, device_id=(g, col_of(zl, lax.rem(y + k, NY), core)), device_id_type=MESH
        )
        return c

    lax.fori_loop(1, NY, greet_y, 0)

    def greet_z(k, c):
        pl.semaphore_signal(
            barrier, inc=1, device_id=(g, col_of(lax.rem(zl + k, NZ), y, core)), device_id_type=MESH
        )
        return c

    lax.fori_loop(1, NZ, greet_z, 0)

    def grp_copy(src, dst, ssem, rsem, k):
        peer = lax.rem(g + k, NG)
        return pltpu.make_async_remote_copy(
            src_ref=src.at[peer], dst_ref=dst.at[g], send_sem=ssem.at[peer], recv_sem=rsem.at[g],
            device_id=(peer, col), device_id_type=MESH,
        )

    def grp_start(src, dst, ssem, rsem):
        def body(k, c):
            grp_copy(src, dst, ssem, rsem, k).start()
            return c

        lax.fori_loop(1, NG, body, 0)

    def grp_wait_recv(src, dst, ssem, rsem):
        def body(k, c):
            peer = lax.rem(g + k, NG)
            pltpu.make_async_remote_copy(
                src_ref=src.at[peer], dst_ref=dst.at[peer], send_sem=ssem.at[peer],
                recv_sem=rsem.at[peer], device_id=(peer, col), device_id_type=MESH,
            ).wait_recv()
            return c

        lax.fori_loop(1, NG, body, 0)

    def grp_wait_send(src, dst, ssem, rsem):
        def body(k, c):
            grp_copy(src, dst, ssem, rsem, k).wait_send()
            return c

        lax.fori_loop(1, NG, body, 0)

    lane = iota((8, ROWS), 1)
    own_c = jnp.zeros((8, ROWS), jnp.int32)
    in_c = lane
    for j in range(NG):
        own_c = jnp.where(lane >= BR * j, own_s[0, j], own_c)
        in_c = jnp.where(lane >= BR * j, lane - BR * j, in_c)
    own_c, in_c = own_c[:1], in_c[:1]
    rows = iota((PROWS, ROWS), 0)
    same = (rows >> 4) == own_c
    in_r = rows & 15
    send_nat = onehot(same & (in_r == in_c))
    send_fold = [onehot(same & (in_r - BR + 4 * b == in_c) & (in_r >= BR)) for b in range(3)]

    def put(i, chunk):
        cs[i] = chunk.reshape(NG, PR, HD)
        cr[i, g] = cs[i, g]

    q = x_ref[:, 2 * HD : 3 * HD]
    put(0, fold_in(send_fold, mm(send_nat, q), x_ref[:, 3 * HD : 3 * HD + 2 * DH]))
    for o in range(NG):
        tile = jnp.zeros((PR, DH), jnp.int32)
        for j in range(NG):
            tile = jnp.where(jnp.full((PR, DH), own_s[0, j]) == o, slot_s[0, j], tile)
        ts[o] = tile.astype(F32)
    tr[g] = ts[g]

    pl.semaphore_wait(barrier, NG - 1 + 1 + NY - 1 + NZ - 1)

    grp_start(ts, tr, t_ssem, t_rsem)
    grp_start(cs.at[0], cr.at[0], c_ssem.at[0], c_rsem.at[0])
    nat = jnp.concatenate([x_ref[:, 3 * HD + 2 * DH : 4 * HD], x_ref[:, HD : HD + 2 * DH]], axis=1)
    put(1, fold_in(send_fold, mm(send_nat, nat), x_ref[:, HD + 2 * DH : HD + 4 * DH]))
    grp_start(cs.at[1], cr.at[1], c_ssem.at[1], c_rsem.at[1])
    branch = mm_nt(og_ref[...], w_ref[...]).astype(BF).astype(F32)
    gate = x_ref[:, :HD].astype(F32)
    grad = (branch * gate).astype(BF)
    put(2, fold_in(send_fold, mm(send_nat, grad), x_ref[:, HD + 4 * DH : 2 * HD]))
    grp_start(cs.at[2], cr.at[2], c_ssem.at[2], c_rsem.at[2])

    rows = iota((PROWS, PROWS), 0)
    cols = iota((PROWS, PROWS), 1)
    same = (rows >> 4) == (cols >> 4)
    rr_, cc_ = rows & 15, cols & 15
    unfold = [onehot(same & (cc_ >= BR) & (rr_ == cc_ - BR + 4 * b)) for b in range(3)]
    infold = [onehot(same & (rr_ >= BR) & (cc_ == rr_ - BR + 4 * b)) for b in range(3)]

    rows = iota((ROWS, PROWS), 0)
    cols = iota((ROWS, PROWS), 1)
    own_r = jnp.zeros((ROWS, PROWS), jnp.int32)
    in_b = rows
    for j in range(NG):
        own_r = jnp.where(rows >= BR * j, own_s[0, j], own_r)
        in_b = jnp.where(rows >= BR * j, rows - BR * j, in_b)
    same = own_r == (cols >> 4)
    cc_ = cols & 15
    home_nat = onehot(same & (cc_ == in_b))
    home_fold = [onehot(same & (cc_ >= BR) & (cc_ - BR + 4 * b == in_b)) for b in range(3)]

    grp_wait_recv(ts, tr, t_ssem, t_rsem)
    slot_r = tr[...].reshape(PROWS, DH)
    lane = iota((8, PROWS), 1)
    slot_c = jnp.zeros((8, PROWS), F32)
    for d in range(NG):
        slot_c = jnp.where((lane >> 4) == d, tr[d, :8, :1], slot_c)
    first = jnp.int32(0)
    length = jnp.int32(1)
    first_r, len_r = jnp.zeros((PROWS, DH), F32), jnp.ones((PROWS, DH), F32)
    first_c = jnp.zeros((8, PROWS), F32)
    for s in range(NG):
        start = len_s[0, s]
        opened = start > 0
        first = jnp.where(opened, s, first)
        length = jnp.where(opened, start, length)
        first_f, length_f = first.astype(F32), length.astype(F32)
        first_r = jnp.where(slot_r == float(s), first_f, first_r)
        len_r = jnp.where(slot_r == float(s), length_f, len_r)
        first_c = jnp.where(slot_c == float(s), first_f, first_c)
    sub = iota((PROWS, DH), 0) & 15
    pos_r = (slot_r - first_r) * BR + sub.astype(F32)
    valid_r = (pos_r < len_r) & (sub < BR)
    pos_c = (slot_c - first_c) * BR + (lane & 15).astype(F32)
    pos_c = jnp.where((lane & 15) < BR, pos_c, 1e9)
    inv_r = jnp.where(valid_r, 1.0 / len_r, 0.0)
    valid = jnp.where(valid_r, 1.0, 0.0)[:, :1]
    weight = jnp.where(
        (first_r[:, :1] == first_c[:1]) & (pos_c[:1] <= pos_r[:, :1]), inv_r[:, :1], 0.0
    )

    scale = 1.0 / math.sqrt(DH)

    def chunk_in(i):
        grp_wait_recv(cs.at[i], cr.at[i], c_ssem.at[i], c_rsem.at[i])
        return cr[i].reshape(PROWS, HD)

    c0 = chunk_in(0)
    k01 = fold_out(unfold, c0).astype(BF)
    qs = [c0[:, head(h)] for h in range(HEADS)]

    def scores(h, kh):
        s = mm_nt(qs[h], kh) * scale
        sig = jax.nn.sigmoid(s)
        p_scr[h] = (s * sig * weight).astype(BF)
        f_scr[h] = sig * (1.0 + s * (1.0 - sig)) * weight

    scores(0, k01[:, :DH])
    scores(1, k01[:, DH:])
    c1 = chunk_in(1)
    ks = [k01[:, :DH], k01[:, DH:]] + [c1[:, head(h)] for h in range(4)]
    for h in range(2, HEADS):
        scores(h, ks[h])
    v23 = fold_out(unfold, c1).astype(BF)
    vs = [c1[:, head(4)], c1[:, head(5)], v23[:, :DH], v23[:, DH:]]
    attended = [mm(p_scr[h], vs[h]) for h in range(4)]
    c2 = chunk_in(2)
    v45 = fold_out(unfold, c2).astype(BF)
    vs += [v45[:, :DH], v45[:, DH:]]
    attended += [mm(p_scr[h], vs[h]) for h in range(4, HEADS)]
    att = jnp.concatenate(attended, axis=1)
    centre = jnp.mean(att, axis=1, keepdims=True)
    att = att - centre
    rstd = lax.rsqrt(jnp.mean(att * att, axis=1, keepdims=True) + 1e-05)
    normed = att * rstd

    gr = c2.astype(F32)
    datt = rstd * (
        gr - jnp.mean(gr, axis=1, keepdims=True)
        - normed * jnp.mean(gr * normed, axis=1, keepdims=True)
    )
    datt = jnp.where(valid > 0.5, datt, 0.0).astype(BF)

    def back(i, natural, pair):
        rs[i] = fold_in(infold, natural, pair.astype(BF)).reshape(NG, PR, HD)
        rr[i, g] = rs[i, g]
        grp_start(rs.at[i], rr.at[i], r_ssem.at[i], r_rsem.at[i])

    def dv(h):
        return mm_tn(p_scr[h], datt[:, head(h)])

    back(0, normed, jnp.concatenate([dv(0), dv(1)], axis=1))

    def dqk(h):
        ds = (mm_nt(datt[:, head(h)], vs[h]) * f_scr[h]).astype(BF)
        return [mm(ds, ks[h]) * scale, mm_tn(ds, qs[h]) * scale]

    back(1, jnp.concatenate(dqk(0) + dqk(1) + dqk(2), axis=1), jnp.concatenate([dv(2), dv(3)], axis=1))
    back(2, jnp.concatenate(dqk(3) + dqk(4) + dqk(5), axis=1), jnp.concatenate([dv(4), dv(5)], axis=1))

    def chunk_home(i):
        grp_wait_recv(rs.at[i], rr.at[i], r_ssem.at[i], r_rsem.at[i])
        chunk = rr[i].reshape(PROWS, HD)
        return mm(home_nat, chunk), chunk

    n_home, chunk = chunk_home(0)
    branch = mm_nt(og_ref[...], w_ref[...]).astype(BF).astype(F32)
    z = (n_home * gate).astype(BF)

    dwf[...] = mm_tn(og_ref[...], z).reshape(NZ, NY, NC, 8, HD)
    for yy in range(NY):
        d1s[yy] = jnp.concatenate([dwf[zz, yy, 1 - core] for zz in range(NZ)], axis=0).astype(BF)
    d1 = pltpu.make_async_remote_copy(
        src_ref=d1s, dst_ref=d1r, send_sem=d1_ssem, recv_sem=d1_rsem,
        device_id=(g, other), device_id_type=MESH,
    )
    d1.start()
    pg_ref[:, :HD] = (branch * n_home).astype(BF)
    pg_ref[:, HD : HD + 2 * DH] = fold_out(home_fold, chunk).astype(BF)
    bo_ref[...] = mm(z, w_ref[...]).astype(BF)
    d1.wait_recv()
    for yy in range(NY):
        mine = jnp.concatenate([dwf[zz, yy, core] for zz in range(NZ)], axis=0)
        d2s[yy] = (mine + d1r[yy].astype(F32)).astype(BF)

    def d2(k, slot):
        peer = lax.rem(y + k, NY)
        return pltpu.make_async_remote_copy(
            src_ref=d2s.at[peer], dst_ref=d2r.at[peer if slot else y], send_sem=d2_ssem.at[peer],
            recv_sem=d2_rsem.at[peer if slot else y],
            device_id=(g, col_of(zl, peer, core)), device_id_type=MESH,
        )

    def d2_start(k, c):
        d2(k, False).start()
        return c

    lax.fori_loop(1, NY, d2_start, 0)
    d2r[y] = d2s[y]

    back1, chunk = chunk_home(1)
    back1 = back1.astype(BF)
    for h in range(3):
        pg_ref[:, 2 * HD + h * DH : 2 * HD + (h + 1) * DH] = back1[:, head(2 * h)]
        pg_ref[:, 3 * HD + h * DH : 3 * HD + (h + 1) * DH] = back1[:, head(2 * h + 1)]
    pg_ref[:, HD + 2 * DH : HD + 4 * DH] = fold_out(home_fold, chunk).astype(BF)

    def d2_wait(k, c):
        d2(k, True).wait_recv()
        return c

    lax.fori_loop(1, NY, d2_wait, 0)
    total = d2r[0].astype(F32)
    for yy in range(1, NY):
        total = total + d2r[yy].astype(F32)
    d3s[...] = total.reshape(NZ, 8, HD)

    def d3(k, slot):
        peer = lax.rem(zl + k, NZ)
        return pltpu.make_async_remote_copy(
            src_ref=d3s.at[peer], dst_ref=d3r.at[peer if slot else zl], send_sem=d3_ssem.at[peer],
            recv_sem=d3_rsem.at[peer if slot else zl],
            device_id=(g, col_of(peer, y, core)), device_id_type=MESH,
        )

    def d3_start(k, c):
        d3(k, False).start()
        return c

    lax.fori_loop(1, NZ, d3_start, 0)
    d3r[zl] = d3s[zl]

    def d3_wait(k, c):
        d3(k, True).wait_recv()
        return c

    lax.fori_loop(1, NZ, d3_wait, 0)
    total = d3r[0] + d3r[1] + d3r[2] + d3r[3]
    for o in range(NG):
        d4s[o, :, :64] = total[:, 64 * o : 64 * o + 64]
        d4s[o, :, 64:] = jnp.zeros((8, 64), F32)
    grp_start(d4s, d4r, d4_ssem, d4_rsem)
    d4r[g] = d4s[g]

    back2, chunk = chunk_home(2)
    back2 = back2.astype(BF)
    for h in range(3):
        pg_ref[:, 2 * HD + (h + 3) * DH : 2 * HD + (h + 4) * DH] = back2[:, head(2 * h)]
        pg_ref[:, 3 * HD + (h + 3) * DH : 3 * HD + (h + 4) * DH] = back2[:, head(2 * h + 1)]
    pg_ref[:, HD + 4 * DH : 2 * HD] = fold_out(home_fold, chunk).astype(BF)

    grp_wait_recv(d4s, d4r, d4_ssem, d4_rsem)
    total = d4r[0]
    for o in range(1, NG):
        total = total + d4r[o]
    dw_ref[...] = jnp.transpose(total)[:64, :]

    grp_wait_send(ts, tr, t_ssem, t_rsem)
    for i in range(3):
        grp_wait_send(cs.at[i], cr.at[i], c_ssem.at[i], c_rsem.at[i])
        grp_wait_send(rs.at[i], rr.at[i], r_ssem.at[i], r_rsem.at[i])
    d1.wait_send()

    def d2_sent(k, c):
        d2(k, False).wait_send()
        return c

    lax.fori_loop(1, NY, d2_sent, 0)

    def d3_sent(k, c):
        d3(k, False).wait_send()
        return c

    lax.fori_loop(1, NZ, d3_sent, 0)
    grp_wait_send(d4s, d4r, d4_ssem, d4_rsem)


def per_device(projected, out_grad, w_out, owners, slots, lengths):
    dma = pltpu.SemaphoreType.DMA
    vmem = pl.BlockSpec(memory_space=pltpu.VMEM)
    smem = pl.BlockSpec(memory_space=pltpu.SMEM)
    bo, pg, dw = pl.pallas_call(
        kernel,
        out_shape=(
            jax.ShapeDtypeStruct((ROWS, 512), BF),
            jax.ShapeDtypeStruct((ROWS, 4 * HD), BF),
            jax.ShapeDtypeStruct((64, 8), F32),
        ),
        in_specs=[smem, smem, smem, vmem, vmem, vmem],
        out_specs=(vmem, vmem, vmem),
        scratch_shapes=[
            pltpu.VMEM((3, NG, PR, HD), BF),
            pltpu.VMEM((3, NG, PR, HD), BF),
            pltpu.VMEM((3, NG, PR, HD), BF),
            pltpu.VMEM((3, NG, PR, HD), BF),
            pltpu.VMEM((NG, PR, DH), F32),
            pltpu.VMEM((NG, PR, DH), F32),
            pltpu.VMEM((HEADS, PROWS, PROWS), BF),
            pltpu.VMEM((HEADS, PROWS, PROWS), F32),
            pltpu.VMEM((NZ, NY, NC, 8, HD), F32),
            pltpu.VMEM((NY, 32, HD), BF),
            pltpu.VMEM((NY, 32, HD), BF),
            pltpu.VMEM((NY, 32, HD), BF),
            pltpu.VMEM((NY, 32, HD), BF),
            pltpu.VMEM((NZ, 8, HD), F32),
            pltpu.VMEM((NZ, 8, HD), F32),
            pltpu.VMEM((NG, 8, DH), F32),
            pltpu.VMEM((NG, 8, DH), F32),
            dma((3, NG)), dma((3, NG)), dma((3, NG)), dma((3, NG)), dma((NG,)), dma((NG,)),
            dma, dma, dma((NY,)), dma((NY,)), dma((NZ,)), dma((NZ,)), dma((NG,)), dma((NG,)),
        ],
        compiler_params=pltpu.CompilerParams(
            collective_id=0, has_side_effects=True, vmem_limit_bytes=48 * 1024 * 1024
        ),
    )(owners, slots, lengths, projected[0], out_grad[0], w_out)
    return (bo[None], pg[None], dw)


def solution(mesh):
    return jax.shard_map(
        per_device,
        mesh=mesh,
        in_specs=(
            P("col", "grp", None),
            P("col", "grp", None),
            P(),
            P("col", "grp"),
            P("col", "grp"),
            P("col", "grp"),
        ),
        out_specs=(P("col", "grp", None), P("col", "grp", None), P("grp", "col")),
        check_vma=False,
    )
```

```python
import functools
import math

import jax
import jax.numpy as jnp
from jax import lax
from jax.experimental import pallas as pl
from jax.experimental.pallas import tpu as pltpu
from jax.sharding import PartitionSpec as P

DH = 128
HEADS = 6
HD = 768
BR = 12
PR = 16
NG = 12
NX, NH = 4, 3
NZ, NY, NC = 4, 8, 2
ROWS = BR * NG
PROWS = PR * NG
MESH = pl.DeviceIdType.MESH
BF = jnp.bfloat16
F32 = jnp.float32


def mm(a, b):
    return lax.dot_general(a, b, (((1,), (0,)), ((), ())), preferred_element_type=F32)


def mm_nt(a, b):
    return lax.dot_general(a, b, (((1,), (1,)), ((), ())), preferred_element_type=F32)


def mm_tn(a, b):
    return lax.dot_general(a, b, (((0,), (0,)), ((), ())), preferred_element_type=F32)


def onehot(cond):
    return jnp.where(cond, 1.0, 0.0).astype(BF)


def iota(shape, dim):
    return lax.broadcasted_iota(jnp.int32, shape, dim)


def fold_in(mats, natural, folded):
    parts = [mm(mats[b], folded) for b in range(3)]
    count = folded.shape[1] // DH
    extra = [parts[b][:, head(m)] for m in range(count) for b in range(3)]
    wide = 3 * DH * count
    done = natural[:, :wide] + jnp.concatenate(extra, axis=1)
    if natural.shape[1] > wide:
        done = jnp.concatenate([done, natural[:, wide:]], axis=1)
    return done.astype(BF)


def fold_out(mats, chunk, count):
    total = None
    for b in range(3):
        lanes = [chunk[:, head(3 * m + b)] for m in range(count)]
        term = mm(mats[b], lanes[0] if count == 1 else jnp.concatenate(lanes, axis=1))
        total = term if total is None else total + term
    return total


def head(h):
    return slice(h * DH, (h + 1) * DH)


def kernel(
    own_s, slot_s, len_s, x_hbm, og_hbm, w_hbm,
    bo_ref, pg_ref, dw_ref, x_ref, og_ref, w_ref, in_sem,
    c0s, c1s, c2s, c3s, c0r, c1r, c2r, c3r, r0s, r1s, r2s, r0r, r1r, r2r,
    ts, tr, p_scr, f_scr, ogt_ref, d1s, d1r, d2s, d2r, d3s, d3r, d4s, d4r,
    c_ssem, c_rsem, r_ssem, r_rsem, t_ssem, t_rsem,
    d1_ssem, d1_rsem, d2_ssem, d2_rsem, d3_ssem, d3_rsem, d4_ssem, d4_rsem,
):
    g = lax.axis_index("grp")
    col = lax.axis_index("col")
    gx, gz = g // NH, lax.rem(g, NH)
    cs, cr = (c0s, c1s, c2s, c3s), (c0r, c1r, c2r, c3r)
    rs, rr = (r0s, r1s, r2s), (r0r, r1r, r2r)
    core = lax.rem(col, NC)
    y = lax.rem(col // NC, NY)
    zl = col // (NC * NY)

    def col_of(z_, y_, c_):
        return (z_ * NY + y_) * NC + c_

    other = col_of(zl, y, 1 - core)

    half = 2 * HD
    loads = [
        pltpu.make_async_copy(x_hbm.at[:, half:], x_ref.at[:, half:], in_sem.at[0]),
        pltpu.make_async_copy(x_hbm.at[:, :half], x_ref.at[:, :half], in_sem.at[1]),
        pltpu.make_async_copy(og_hbm, og_ref, in_sem.at[2]),
        pltpu.make_async_copy(w_hbm, w_ref, in_sem.at[3]),
    ]

    barrier = pltpu.get_barrier_semaphore()

    def greet(k, c):
        pl.semaphore_signal(
            barrier, inc=1, device_id=(lax.rem(g + k, NG), col), device_id_type=MESH
        )
        return c

    lax.fori_loop(1, NG, greet, 0)
    pl.semaphore_signal(barrier, inc=1, device_id=(g, other), device_id_type=MESH)

    def greet_y(k, c):
        pl.semaphore_signal(
            barrier, inc=1, device_id=(g, col_of(zl, lax.rem(y + k, NY), core)), device_id_type=MESH
        )
        return c

    lax.fori_loop(1, NY, greet_y, 0)

    def z_peer(k):
        place = lax.rem(zl * NH + gz + k, NG)
        return place, (gx * NH + lax.rem(place, NH), col_of(place // NH, y, core))

    def greet_z(k, c):
        pl.semaphore_signal(barrier, inc=1, device_id=z_peer(k)[1], device_id_type=MESH)
        return c

    lax.fori_loop(1, NG, greet_z, 0)
    for load in loads:
        load.start()

    def grp_copy(src, dst, ssem, rsem, k):
        peer = lax.rem(g + k, NG)
        return pltpu.make_async_remote_copy(
            src_ref=src.at[peer], dst_ref=dst.at[g], send_sem=ssem.at[peer], recv_sem=rsem.at[g],
            device_id=(peer, col), device_id_type=MESH,
        )

    def grp_start(src, dst, ssem, rsem):
        def body(k, c):
            grp_copy(src, dst, ssem, rsem, k).start()
            return c

        lax.fori_loop(1, NG, body, 0)

    def grp_wait_recv(src, dst, ssem, rsem):
        def body(k, c):
            peer = lax.rem(g + k, NG)
            pltpu.make_async_remote_copy(
                src_ref=src.at[peer], dst_ref=dst.at[peer], send_sem=ssem.at[peer],
                recv_sem=rsem.at[peer], device_id=(peer, col), device_id_type=MESH,
            ).wait_recv()
            return c

        lax.fori_loop(1, NG, body, 0)

    def grp_wait_send(src, dst, ssem, rsem):
        def body(k, c):
            grp_copy(src, dst, ssem, rsem, k).wait_send()
            return c

        lax.fori_loop(1, NG, body, 0)

    lane = iota((8, ROWS), 1)
    own_c = jnp.zeros((8, ROWS), jnp.int32)
    in_c = lane
    for j in range(NG):
        own_c = jnp.where(lane >= BR * j, own_s[0, j], own_c)
        in_c = jnp.where(lane >= BR * j, lane - BR * j, in_c)
    own_c, in_c = own_c[:1], in_c[:1]
    rows = iota((PROWS, ROWS), 0)
    same = (rows >> 4) == own_c
    in_r = rows & 15
    send_nat = onehot(same & (in_r == in_c))
    send_fold = [onehot(same & (in_r - BR + 4 * b == in_c) & (in_r >= BR)) for b in range(3)]

    def put(i, chunk):
        cs[i][...] = chunk.reshape(NG, PR, chunk.shape[1])
        cr[i][g] = cs[i][g]

    def send(i):
        grp_start(cs[i], cr[i], c_ssem.at[i], c_rsem.at[i])

    loads[0].wait()
    q = x_ref[:, 2 * HD : 3 * HD]
    put(0, fold_in(send_fold, mm(send_nat, q), x_ref[:, 3 * HD : 3 * HD + 2 * DH]))
    for o in range(NG):
        tile = jnp.zeros((1, DH), jnp.int32)
        for j in range(NG):
            tile = jnp.where(jnp.full((1, DH), own_s[0, j]) == o, slot_s[0, j], tile)
        ts[o] = tile.astype(F32)
    tr[g] = ts[g]

    pl.semaphore_wait(barrier, NG - 1 + 1 + NY - 1 + NG - 1)

    grp_start(ts, tr, t_ssem, t_rsem)
    send(0)
    loads[1].wait()
    nat = jnp.concatenate([x_ref[:, 3 * HD + 2 * DH : 4 * HD], x_ref[:, HD : HD + 2 * DH]], axis=1)
    put(1, fold_in(send_fold, mm(send_nat, nat), x_ref[:, HD + 2 * DH : HD + 4 * DH]))
    send(1)
    loads[2].wait()
    loads[3].wait()
    branch = mm_nt(og_ref[...], w_ref[...]).astype(BF).astype(F32)
    gate = x_ref[:, :HD].astype(F32)
    grad = (branch * gate).astype(BF)
    put(
        2,
        fold_in(
            send_fold,
            mm(send_nat, jnp.concatenate([x_ref[:, HD + 4 * DH : half], grad[:, head(0)]], axis=1)),
            grad[:, head(1)],
        ),
    )
    send(2)
    put(3, fold_in(send_fold, mm(send_nat, grad[:, 2 * DH : 5 * DH]), grad[:, head(5)]))
    send(3)

    ogt = jnp.transpose(og_ref[...].astype(F32))
    for cc in range(NC):
        ogt_ref[cc] = jnp.concatenate(
            [
                ogt[((zz * NY + yy) * NC + cc) * 8 : ((zz * NY + yy) * NC + cc) * 8 + 8]
                for yy in range(NY)
                for zz in range(NZ)
            ],
            axis=0,
        ).astype(BF)

    rows = iota((PROWS, PROWS), 0)
    cols = iota((PROWS, PROWS), 1)
    same = (rows >> 4) == (cols >> 4)
    rr_, cc_ = rows & 15, cols & 15
    unfold = [onehot(same & (cc_ >= BR) & (rr_ == cc_ - BR + 4 * b)) for b in range(3)]
    infold = [onehot(same & (rr_ >= BR) & (cc_ == rr_ - BR + 4 * b)) for b in range(3)]

    rows = iota((ROWS, PROWS), 0)
    cols = iota((ROWS, PROWS), 1)
    own_r = jnp.zeros((ROWS, PROWS), jnp.int32)
    in_b = rows
    for j in range(NG):
        own_r = jnp.where(rows >= BR * j, own_s[0, j], own_r)
        in_b = jnp.where(rows >= BR * j, rows - BR * j, in_b)
    same = own_r == (cols >> 4)
    cc_ = cols & 15
    home_nat = onehot(same & (cc_ == in_b))
    home_fold = [onehot(same & (cc_ >= BR) & (cc_ - BR + 4 * b == in_b)) for b in range(3)]

    grp_wait_recv(ts, tr, t_ssem, t_rsem)
    slot_r = jnp.concatenate([jnp.broadcast_to(tr[d], (PR, DH)) for d in range(NG)], axis=0)
    lane = iota((8, PROWS), 1)
    slot_c = jnp.zeros((8, PROWS), F32)
    for d in range(NG):
        slot_c = jnp.where((lane >> 4) == d, jnp.broadcast_to(tr[d][:, :1], (8, PROWS)), slot_c)
    first = jnp.int32(0)
    length = jnp.int32(1)
    first_r, len_r = jnp.zeros((PROWS, DH), F32), jnp.ones((PROWS, DH), F32)
    first_c = jnp.zeros((8, PROWS), F32)
    for s in range(NG):
        start = len_s[0, s]
        opened = start > 0
        first = jnp.where(opened, s, first)
        length = jnp.where(opened, start, length)
        first_f, length_f = first.astype(F32), length.astype(F32)
        first_r = jnp.where(slot_r == float(s), first_f, first_r)
        len_r = jnp.where(slot_r == float(s), length_f, len_r)
        first_c = jnp.where(slot_c == float(s), first_f, first_c)
    sub = iota((PROWS, DH), 0) & 15
    pos_r = (slot_r - first_r) * BR + sub.astype(F32)
    valid_r = (pos_r < len_r) & (sub < BR)
    pos_c = (slot_c - first_c) * BR + (lane & 15).astype(F32)
    pos_c = jnp.where((lane & 15) < BR, pos_c, 1e9)
    inv_r = jnp.where(valid_r, 1.0 / len_r, 0.0)
    valid = jnp.where(valid_r, 1.0, 0.0)[:, :1]
    weight = jnp.where(
        (first_r[:, :1] == first_c[:1]) & (pos_c[:1] <= pos_r[:, :1]), inv_r[:, :1], 0.0
    )

    scale = 1.0 / math.sqrt(DH)

    def chunk_in(i):
        grp_wait_recv(cs[i], cr[i], c_ssem.at[i], c_rsem.at[i])
        return cr[i][...].reshape(PROWS, cr[i].shape[2])

    c0 = chunk_in(0)
    k01 = fold_out(unfold, c0, 2).astype(BF)
    qs = [c0[:, head(h)] for h in range(HEADS)]

    def scores(h, kh):
        s = mm_nt(qs[h], kh) * scale
        sig = jax.nn.sigmoid(s)
        p_scr[h] = (s * sig * weight).astype(BF)
        f_scr[h] = sig * (1.0 + s * (1.0 - sig)) * weight

    scores(0, k01[:, :DH])
    scores(1, k01[:, DH:])
    c1 = chunk_in(1)
    ks = [k01[:, :DH], k01[:, DH:]] + [c1[:, head(h)] for h in range(4)]
    for h in range(2, HEADS):
        scores(h, ks[h])
    v23 = fold_out(unfold, c1, 2).astype(BF)
    vs = [c1[:, head(4)], c1[:, head(5)], v23[:, :DH], v23[:, DH:]]
    attended = [mm(p_scr[h], vs[h]) for h in range(4)]
    c2 = chunk_in(2)
    grad1 = fold_out(unfold, c2, 1)
    vs += [c2[:, head(0)], c2[:, head(1)]]
    attended += [mm(p_scr[h], vs[h]) for h in range(4, HEADS)]
    att = jnp.concatenate(attended, axis=1)
    centre = jnp.mean(att, axis=1, keepdims=True)
    att = att - centre
    rstd = lax.rsqrt(jnp.mean(att * att, axis=1, keepdims=True) + 1e-05)
    normed = att * rstd

    def back(i, natural, folded):
        rs[i][...] = fold_in(infold, natural, folded.astype(BF)).reshape(NG, PR, natural.shape[1])
        rr[i][g] = rs[i][g]

    def back_start(i):
        grp_start(rs[i], rr[i], r_ssem.at[i], r_rsem.at[i])

    def back_chain(i):
        def body(k, c):
            grp_copy(rs[i - 1], rr[i - 1], r_ssem.at[i - 1], r_rsem.at[i - 1], k).wait_send()
            grp_copy(rs[i], rr[i], r_ssem.at[i], r_rsem.at[i], k).start()
            return c

        lax.fori_loop(1, NG, body, 0)

    def back_sent(i):
        grp_wait_send(rs[i], rr[i], r_ssem.at[i], r_rsem.at[i])

    back(0, jnp.concatenate([normed[:, : 3 * DH], normed[:, 4 * DH :]], axis=1), normed[:, head(3)])

    back_start(0)

    c3 = chunk_in(3)
    gr = jnp.concatenate(
        [c2[:, head(2)].astype(F32), grad1, c3.astype(F32), fold_out(unfold, c3, 1)], axis=1
    )
    datt = rstd * (
        gr - jnp.mean(gr, axis=1, keepdims=True)
        - normed * jnp.mean(gr * normed, axis=1, keepdims=True)
    )
    datt = jnp.where(valid > 0.5, datt, 0.0).astype(BF)

    def dv(h):
        return mm_tn(p_scr[h], datt[:, head(h)])

    def dqk(h):
        ds = (mm_nt(datt[:, head(h)], vs[h]) * f_scr[h]).astype(BF)
        return [mm(ds, ks[h]) * scale, mm_tn(ds, qs[h]) * scale]

    for i in (1, 2):
        a = 3 * (i - 1)
        natural = dqk(a) + dqk(a + 1) + dqk(a + 2) + [dv(a)]
        back(i, jnp.concatenate(natural, axis=1), jnp.concatenate([dv(a + 1), dv(a + 2)], axis=1))
        if i == 1:
            back_chain(1)

    def chunk_home(i):
        grp_wait_recv(rs[i], rr[i], r_ssem.at[i], r_rsem.at[i])
        chunk = rr[i][...].reshape(PROWS, rr[i].shape[2])
        return mm(home_nat, chunk), chunk

    n_part, chunk = chunk_home(0)
    n_home = jnp.concatenate(
        [n_part[:, : 3 * DH], fold_out(home_fold, chunk, 1), n_part[:, 3 * DH :]], axis=1
    )
    z = (n_home * gate).astype(BF)

    zc = jnp.concatenate(
        [z[:, 192 * xx : 192 * xx + DH] for xx in range(NX)]
        + [z[:, 192 * xx + DH : 192 * xx + 192] for xx in range(NX)],
        axis=1,
    )
    d1s[...] = mm(ogt_ref[1 - core], zc).astype(BF)
    d1 = pltpu.make_async_remote_copy(
        src_ref=d1s, dst_ref=d1r, send_sem=d1_ssem, recv_sem=d1_rsem,
        device_id=(g, other), device_id_type=MESH,
    )
    d1.start()
    own = mm(ogt_ref[core], zc)
    d1.wait_recv()
    mine = (own + d1r[...].astype(F32)).astype(BF)
    for xx in range(NX):
        d2s[xx, :256] = mine[:, head(xx)]
        tail = mine[:, 512 + 64 * xx : 576 + 64 * xx]
        d2s[xx, 256:] = jnp.concatenate([tail[:128], tail[128:]], axis=1)

    def d2(k, slot):
        peer = lax.rem(gx + k, NX)
        return pltpu.make_async_remote_copy(
            src_ref=d2s.at[peer], dst_ref=d2r.at[peer if slot else gx], send_sem=d2_ssem.at[peer],
            recv_sem=d2_rsem.at[peer if slot else gx],
            device_id=(peer * NH + gz, col), device_id_type=MESH,
        )

    def d2_start(k, c):
        d2(k, False).start()
        return c

    lax.fori_loop(1, NX, d2_start, 0)
    back_chain(2)
    d2r[gx] = d2s[gx]
    branch = mm_nt(og_ref[...], w_ref[...]).astype(BF).astype(F32)
    pg_ref[:, :HD] = (branch * n_home).astype(BF)
    bo_ref[...] = mm(z, w_ref[...]).astype(BF)

    def d2_wait(k, c):
        d2(k, True).wait_recv()
        return c

    lax.fori_loop(1, NX, d2_wait, 0)
    total = d2r[0].astype(F32)
    for xx in range(1, NX):
        total = total + d2r[xx].astype(F32)
    for yy in range(NY):
        d3s[yy, :32] = total[32 * yy : 32 * yy + 32].astype(BF)
        row, lane0 = 256 + 32 * (yy % 4), 64 * (yy // 4)
        tail = total[row : row + 32, lane0 : lane0 + 64]
        d3s[yy, 32:] = jnp.concatenate([tail[:16], tail[16:]], axis=1).astype(BF)

    def d3(k, slot):
        peer = lax.rem(y + k, NY)
        return pltpu.make_async_remote_copy(
            src_ref=d3s.at[peer], dst_ref=d3r.at[peer if slot else y], send_sem=d3_ssem.at[peer],
            recv_sem=d3_rsem.at[peer if slot else y],
            device_id=(g, col_of(zl, peer, core)), device_id_type=MESH,
        )

    def d3_start(k, c):
        d3(k, False).start()
        return c

    lax.fori_loop(1, NY, d3_start, 0)
    d3r[y] = d3s[y]

    def d3_wait(k, c):
        d3(k, True).wait_recv()
        return c

    lax.fori_loop(1, NY, d3_wait, 0)
    total = d3r[0].astype(F32)
    for yy in range(1, NY):
        total = total + d3r[yy].astype(F32)
    for zz in range(NZ):
        for hh in range(NH):
            row, lane0 = (8 * zz, 64 * hh) if hh < 2 else (32 + 8 * (zz % 2), 64 * (zz // 2))
            d4s[zz * NH + hh, :, :64] = total[row : row + 8, lane0 : lane0 + 64]
            d4s[zz * NH + hh, :, 64:] = jnp.zeros((8, 64), F32)
    place = zl * NH + gz

    def d4(k, slot):
        peer, device = z_peer(k)
        return pltpu.make_async_remote_copy(
            src_ref=d4s.at[peer], dst_ref=d4r.at[peer if slot else place], send_sem=d4_ssem.at[peer],
            recv_sem=d4_rsem.at[peer if slot else place], device_id=device, device_id_type=MESH,
        )

    def d4_start(k, c):
        d4(k, False).start()
        return c

    lax.fori_loop(1, NG, d4_start, 0)
    d4r[place] = d4s[place]

    for i in (1, 2):
        a = 3 * (i - 1)
        part, chunk = chunk_home(i)
        part = part.astype(BF)
        for h in range(3):
            lo = 2 * HD + (a + h) * DH
            pg_ref[:, lo : lo + DH] = part[:, head(2 * h)]
            pg_ref[:, lo + HD : lo + HD + DH] = part[:, head(2 * h + 1)]
        lo = HD + a * DH
        pg_ref[:, lo : lo + DH] = part[:, head(6)]
        pg_ref[:, lo + DH : lo + 3 * DH] = fold_out(home_fold, chunk, 2).astype(BF)

    def d4_wait(k, c):
        d4(k, True).wait_recv()
        return c

    lax.fori_loop(1, NG, d4_wait, 0)
    total = d4r[0]
    for o in range(1, NG):
        total = total + d4r[o]
    dw_ref[...] = total[:, :64]

    grp_wait_send(ts, tr, t_ssem, t_rsem)
    for i in range(4):
        grp_wait_send(cs[i], cr[i], c_ssem.at[i], c_rsem.at[i])
    back_sent(2)
    d1.wait_send()

    def d2_sent(k, c):
        d2(k, False).wait_send()
        return c

    lax.fori_loop(1, NX, d2_sent, 0)

    def d3_sent(k, c):
        d3(k, False).wait_send()
        return c

    lax.fori_loop(1, NY, d3_sent, 0)

    def d4_sent(k, c):
        d4(k, False).wait_send()
        return c

    lax.fori_loop(1, NG, d4_sent, 0)


def per_device(projected, out_grad, w_out, owners, slots, lengths):
    dma = pltpu.SemaphoreType.DMA
    vmem = pl.BlockSpec(memory_space=pltpu.VMEM)
    hbm = pl.BlockSpec(memory_space=pltpu.HBM)
    smem = pl.BlockSpec(memory_space=pltpu.SMEM)
    bo, pg, dw = pl.pallas_call(
        kernel,
        out_shape=(
            jax.ShapeDtypeStruct((ROWS, 512), BF),
            jax.ShapeDtypeStruct((ROWS, 4 * HD), BF),
            jax.ShapeDtypeStruct((8, 64), F32),
        ),
        in_specs=[smem, smem, smem, hbm, hbm, hbm],
        out_specs=(vmem, vmem, vmem),
        scratch_shapes=[
            pltpu.VMEM((ROWS, 4 * HD), BF),
            pltpu.VMEM((ROWS, 512), BF),
            pltpu.VMEM((HD, 512), BF),
            dma((4,)),
            *[pltpu.VMEM((NG, PR, w), BF) for w in (768, 768, 384, 384) * 2 + (640, 896, 896) * 2],
            pltpu.VMEM((NG, 1, DH), F32),
            pltpu.VMEM((NG, 1, DH), F32),
            pltpu.VMEM((HEADS, PROWS, PROWS), BF),
            pltpu.VMEM((HEADS, PROWS, PROWS), F32),
            pltpu.VMEM((NC, 256, ROWS), BF),
            pltpu.VMEM((256, HD), BF),
            pltpu.VMEM((256, HD), BF),
            pltpu.VMEM((NX, 384, DH), BF),
            pltpu.VMEM((NX, 384, DH), BF),
            pltpu.VMEM((NY, 48, DH), BF),
            pltpu.VMEM((NY, 48, DH), BF),
            pltpu.VMEM((NG, 8, DH), F32),
            pltpu.VMEM((NG, 8, DH), F32),
            dma((4, NG)), dma((4, NG)), dma((3, NG)), dma((3, NG)), dma((NG,)), dma((NG,)),
            dma, dma, dma((NX,)), dma((NX,)), dma((NY,)), dma((NY,)), dma((NG,)), dma((NG,)),
        ],
        compiler_params=pltpu.CompilerParams(
            collective_id=0, has_side_effects=True, vmem_limit_bytes=63 * 1024 * 1024
        ),
    )(owners, slots, lengths, projected[0], out_grad[0], w_out)
    return (bo[None], pg[None], dw.T)


def solution(mesh):
    return jax.shard_map(
        per_device,
        mesh=mesh,
        in_specs=(
            P("col", "grp", None),
            P("col", "grp", None),
            P(),
            P("col", "grp"),
            P("col", "grp"),
            P("col", "grp"),
        ),
        out_specs=(P("col", "grp", None), P("col", "grp", None), P("grp", "col")),
        check_vma=False,
    )
```

```python
import functools
import math

import jax
import jax.numpy as jnp
from jax import lax
from jax.experimental import pallas as pl
from jax.experimental.pallas import tpu as pltpu
from jax.sharding import PartitionSpec as P

DH = 128
HEADS = 6
HD = 768
BR = 12
PR = 16
NG = 12
NX, NH = 4, 3
NZ, NY, NC = 4, 8, 2
ROWS = BR * NG
PROWS = PR * NG
MESH = pl.DeviceIdType.MESH
BF = jnp.bfloat16
F32 = jnp.float32


def mm(a, b):
    return lax.dot_general(a, b, (((1,), (0,)), ((), ())), preferred_element_type=F32)


def mm_nt(a, b):
    return lax.dot_general(a, b, (((1,), (1,)), ((), ())), preferred_element_type=F32)


def mm_tn(a, b):
    return lax.dot_general(a, b, (((0,), (0,)), ((), ())), preferred_element_type=F32)


def onehot(cond):
    return jnp.where(cond, 1.0, 0.0).astype(BF)


def iota(shape, dim):
    return lax.broadcasted_iota(jnp.int32, shape, dim)


def fold_in(mats, natural, folded):
    parts = [mm(mats[b], folded) for b in range(3)]
    count = folded.shape[1] // DH
    extra = [parts[b][:, head(m)] for m in range(count) for b in range(3)]
    wide = 3 * DH * count
    done = natural[:, :wide] + jnp.concatenate(extra, axis=1)
    if natural.shape[1] > wide:
        done = jnp.concatenate([done, natural[:, wide:]], axis=1)
    return done.astype(BF)


def fold_out(mats, chunk, count):
    total = None
    for b in range(3):
        lanes = [chunk[:, head(3 * m + b)] for m in range(count)]
        term = mm(mats[b], lanes[0] if count == 1 else jnp.concatenate(lanes, axis=1))
        total = term if total is None else total + term
    return total


def head(h):
    return slice(h * DH, (h + 1) * DH)


def kernel(
    own_s, slot_s, len_s, x_hbm, og_hbm, w_hbm,
    bo_ref, pg_ref, dw_ref, x_ref, og_ref, w_ref, in_sem,
    c0s, c1s, c2s, c3s, c0r, c1r, c2r, c3r, r0s, r1s, r2s, r0r, r1r, r2r,
    ts, tr, p_scr, f_scr, ogt_ref, d1s, d1r, d2s, d2r, d3s, d3r, d4s, d4r,
    c_ssem, c_rsem, r_ssem, r_rsem, t_ssem, t_rsem,
    d1_ssem, d1_rsem, d2_ssem, d2_rsem, d3_ssem, d3_rsem, d4_ssem, d4_rsem,
):
    g = lax.axis_index("grp")
    col = lax.axis_index("col")
    gx, gz = g // NH, lax.rem(g, NH)
    cs, cr = (c0s, c1s, c2s, c3s), (c0r, c1r, c2r, c3r)
    rs, rr = (r0s, r1s, r2s), (r0r, r1r, r2r)
    core = lax.rem(col, NC)
    y = lax.rem(col // NC, NY)
    zl = col // (NC * NY)

    def col_of(z_, y_, c_):
        return (z_ * NY + y_) * NC + c_

    other = col_of(zl, y, 1 - core)

    half = 2 * HD
    loads = [
        pltpu.make_async_copy(x_hbm.at[:, half:], x_ref.at[:, half:], in_sem.at[0]),
        pltpu.make_async_copy(x_hbm.at[:, :half], x_ref.at[:, :half], in_sem.at[1]),
        pltpu.make_async_copy(og_hbm, og_ref, in_sem.at[2]),
        pltpu.make_async_copy(w_hbm, w_ref, in_sem.at[3]),
    ]

    barrier = pltpu.get_barrier_semaphore()

    def greet(k, c):
        pl.semaphore_signal(
            barrier, inc=1, device_id=(lax.rem(g + k, NG), col), device_id_type=MESH
        )
        return c

    lax.fori_loop(1, NG, greet, 0)
    pl.semaphore_signal(barrier, inc=1, device_id=(g, other), device_id_type=MESH)

    def greet_y(k, c):
        pl.semaphore_signal(
            barrier, inc=1, device_id=(g, col_of(zl, lax.rem(y + k, NY), core)), device_id_type=MESH
        )
        return c

    lax.fori_loop(1, NY, greet_y, 0)

    def z_peer(k):
        place = lax.rem(zl * NH + gz + k, NG)
        return place, (gx * NH + lax.rem(place, NH), col_of(place // NH, y, core))

    def greet_z(k, c):
        pl.semaphore_signal(barrier, inc=1, device_id=z_peer(k)[1], device_id_type=MESH)
        return c

    lax.fori_loop(1, NG, greet_z, 0)
    for load in loads:
        load.start()

    def grp_copy(src, dst, ssem, rsem, k):
        peer = lax.rem(g + k, NG)
        return pltpu.make_async_remote_copy(
            src_ref=src.at[peer], dst_ref=dst.at[g], send_sem=ssem.at[peer], recv_sem=rsem.at[g],
            device_id=(peer, col), device_id_type=MESH,
        )

    def grp_start(src, dst, ssem, rsem):
        def body(k, c):
            grp_copy(src, dst, ssem, rsem, k).start()
            return c

        lax.fori_loop(1, NG, body, 0)

    def grp_wait_recv(src, dst, ssem, rsem):
        def body(k, c):
            peer = lax.rem(g + k, NG)
            pltpu.make_async_remote_copy(
                src_ref=src.at[peer], dst_ref=dst.at[peer], send_sem=ssem.at[peer],
                recv_sem=rsem.at[peer], device_id=(peer, col), device_id_type=MESH,
            ).wait_recv()
            return c

        lax.fori_loop(1, NG, body, 0)

    def grp_wait_send(src, dst, ssem, rsem):
        def body(k, c):
            grp_copy(src, dst, ssem, rsem, k).wait_send()
            return c

        lax.fori_loop(1, NG, body, 0)

    lane = iota((8, ROWS), 1)
    own_c = jnp.zeros((8, ROWS), jnp.int32)
    in_c = lane
    for j in range(NG):
        own_c = jnp.where(lane >= BR * j, own_s[0, j], own_c)
        in_c = jnp.where(lane >= BR * j, lane - BR * j, in_c)
    own_c, in_c = own_c[:1], in_c[:1]
    rows = iota((PROWS, ROWS), 0)
    same = (rows >> 4) == own_c
    in_r = rows & 15
    send_nat = onehot(same & (in_r == in_c))
    send_fold = [onehot(same & (in_r - BR + 4 * b == in_c) & (in_r >= BR)) for b in range(3)]

    def put(i, chunk):
        cs[i][...] = chunk.reshape(NG, PR, chunk.shape[1])
        cr[i][g] = cs[i][g]

    def send(i):
        grp_start(cs[i], cr[i], c_ssem.at[i], c_rsem.at[i])

    loads[0].wait()
    q = x_ref[:, 2 * HD : 3 * HD]
    put(0, fold_in(send_fold, mm(send_nat, q), x_ref[:, 3 * HD : 3 * HD + 2 * DH]))
    for o in range(NG):
        tile = jnp.zeros((1, DH), jnp.int32)
        for j in range(NG):
            tile = jnp.where(jnp.full((1, DH), own_s[0, j]) == o, slot_s[0, j], tile)
        ts[o] = tile.astype(F32)
    tr[g] = ts[g]

    pl.semaphore_wait(barrier, NG - 1 + 1 + NY - 1 + NG - 1)

    grp_start(ts, tr, t_ssem, t_rsem)
    send(0)
    loads[1].wait()
    nat = jnp.concatenate([x_ref[:, 3 * HD + 2 * DH : 4 * HD], x_ref[:, HD : HD + 2 * DH]], axis=1)
    put(1, fold_in(send_fold, mm(send_nat, nat), x_ref[:, HD + 2 * DH : HD + 4 * DH]))
    send(1)
    nat = jnp.concatenate([x_ref[:, HD + 4 * DH : half], x_ref[:, :DH]], axis=1)
    put(2, fold_in(send_fold, mm(send_nat, nat), x_ref[:, DH : 2 * DH]))
    send(2)
    loads[2].wait()
    nat = jnp.concatenate([x_ref[:, 2 * DH : HD], og_ref[:, : 2 * DH]], axis=1)
    put(3, fold_in(send_fold, mm(send_nat, nat), og_ref[:, 2 * DH :]))
    send(3)
    loads[3].wait()
    branch = mm_nt(og_ref[...], w_ref[...]).astype(BF).astype(F32)
    gate = x_ref[:, :HD].astype(F32)

    rows = iota((PROWS, PROWS), 0)
    cols = iota((PROWS, PROWS), 1)
    same = (rows >> 4) == (cols >> 4)
    rr_, cc_ = rows & 15, cols & 15
    unfold = [onehot(same & (cc_ >= BR) & (rr_ == cc_ - BR + 4 * b)) for b in range(3)]
    infold = [onehot(same & (rr_ >= BR) & (cc_ == rr_ - BR + 4 * b)) for b in range(3)]

    rows = iota((ROWS, PROWS), 0)
    cols = iota((ROWS, PROWS), 1)
    own_r = jnp.zeros((ROWS, PROWS), jnp.int32)
    in_b = rows
    for j in range(NG):
        own_r = jnp.where(rows >= BR * j, own_s[0, j], own_r)
        in_b = jnp.where(rows >= BR * j, rows - BR * j, in_b)
    same = own_r == (cols >> 4)
    cc_ = cols & 15
    home_nat = onehot(same & (cc_ == in_b))
    home_fold = [onehot(same & (cc_ >= BR) & (cc_ - BR + 4 * b == in_b)) for b in range(3)]

    grp_wait_recv(ts, tr, t_ssem, t_rsem)
    slot_r = jnp.concatenate([jnp.broadcast_to(tr[d], (PR, DH)) for d in range(NG)], axis=0)
    lane = iota((8, PROWS), 1)
    slot_c = jnp.zeros((8, PROWS), F32)
    for d in range(NG):
        slot_c = jnp.where((lane >> 4) == d, jnp.broadcast_to(tr[d][:, :1], (8, PROWS)), slot_c)
    first = jnp.int32(0)
    length = jnp.int32(1)
    first_r, len_r = jnp.zeros((PROWS, DH), F32), jnp.ones((PROWS, DH), F32)
    first_c = jnp.zeros((8, PROWS), F32)
    for s in range(NG):
        start = len_s[0, s]
        opened = start > 0
        first = jnp.where(opened, s, first)
        length = jnp.where(opened, start, length)
        first_f, length_f = first.astype(F32), length.astype(F32)
        first_r = jnp.where(slot_r == float(s), first_f, first_r)
        len_r = jnp.where(slot_r == float(s), length_f, len_r)
        first_c = jnp.where(slot_c == float(s), first_f, first_c)
    sub = iota((PROWS, DH), 0) & 15
    pos_r = (slot_r - first_r) * BR + sub.astype(F32)
    valid_r = (pos_r < len_r) & (sub < BR)
    pos_c = (slot_c - first_c) * BR + (lane & 15).astype(F32)
    pos_c = jnp.where((lane & 15) < BR, pos_c, 1e9)
    inv_r = jnp.where(valid_r, 1.0 / len_r, 0.0)
    valid = jnp.where(valid_r, 1.0, 0.0)[:, :1]
    weight = jnp.where(
        (first_r[:, :1] == first_c[:1]) & (pos_c[:1] <= pos_r[:, :1]), inv_r[:, :1], 0.0
    )

    scale = 1.0 / math.sqrt(DH)

    def chunk_in(i):
        grp_wait_recv(cs[i], cr[i], c_ssem.at[i], c_rsem.at[i])
        return cr[i][...].reshape(PROWS, cr[i].shape[2])

    c0 = chunk_in(0)
    k01 = fold_out(unfold, c0, 2).astype(BF)
    qs = [c0[:, head(h)] for h in range(HEADS)]

    def scores(h, kh):
        s = mm_nt(qs[h], kh) * scale
        sig = jax.nn.sigmoid(s)
        p_scr[h] = (s * sig * weight).astype(BF)
        f_scr[h] = sig * (1.0 + s * (1.0 - sig)) * weight

    scores(0, k01[:, :DH])
    scores(1, k01[:, DH:])
    c1 = chunk_in(1)
    ks = [k01[:, :DH], k01[:, DH:]] + [c1[:, head(h)] for h in range(4)]
    for h in range(2, HEADS):
        scores(h, ks[h])
    v23 = fold_out(unfold, c1, 2).astype(BF)
    vs = [c1[:, head(4)], c1[:, head(5)], v23[:, :DH], v23[:, DH:]]
    attended = [mm(p_scr[h], vs[h]) for h in range(4)]
    c2 = chunk_in(2)
    gate1 = fold_out(unfold, c2, 1)
    vs += [c2[:, head(0)], c2[:, head(1)]]
    attended += [mm(p_scr[h], vs[h]) for h in range(4, HEADS)]
    att = jnp.concatenate(attended, axis=1)
    centre = jnp.mean(att, axis=1, keepdims=True)
    att = att - centre
    rstd = lax.rsqrt(jnp.mean(att * att, axis=1, keepdims=True) + 1e-05)
    normed = att * rstd

    def back(i, natural, folded):
        rs[i][...] = fold_in(infold, natural, folded.astype(BF)).reshape(NG, PR, natural.shape[1])
        rr[i][g] = rs[i][g]

    def back_start(i):
        grp_start(rs[i], rr[i], r_ssem.at[i], r_rsem.at[i])

    back(0, jnp.concatenate([normed[:, : 3 * DH], normed[:, 4 * DH :]], axis=1), normed[:, head(3)])

    back_start(0)

    c3 = chunk_in(3)
    gate_o = jnp.concatenate(
        [c2[:, head(2)].astype(F32), gate1, c3[:, : 4 * DH].astype(F32)], axis=1
    )
    og_o = jnp.concatenate([c3[:, 4 * DH :], fold_out(unfold, c3, 2).astype(BF)], axis=1)

    ogt = jnp.transpose(og_o.astype(F32))
    for cc in range(NC):
        ogt_ref[cc] = jnp.concatenate(
            [
                ogt[((zz * NY + yy) * NC + cc) * 8 : ((zz * NY + yy) * NC + cc) * 8 + 8]
                for yy in range(NY)
                for zz in range(NZ)
            ],
            axis=0,
        ).astype(BF)

    zo = (normed * gate_o).astype(BF)
    d1s[...] = mm(ogt_ref[1 - core], zo).astype(BF)
    d1 = pltpu.make_async_remote_copy(
        src_ref=d1s, dst_ref=d1r, send_sem=d1_ssem, recv_sem=d1_rsem,
        device_id=(g, other), device_id_type=MESH,
    )
    d1.start()

    gr = mm_nt(og_o, w_ref[...]).astype(BF).astype(F32) * gate_o
    datt = rstd * (
        gr - jnp.mean(gr, axis=1, keepdims=True)
        - normed * jnp.mean(gr * normed, axis=1, keepdims=True)
    )
    datt = jnp.where(valid > 0.5, datt, 0.0).astype(BF)

    def dv(h):
        return mm_tn(p_scr[h], datt[:, head(h)])

    def dqk(h):
        ds = (mm_nt(datt[:, head(h)], vs[h]) * f_scr[h]).astype(BF)
        return [mm(ds, ks[h]) * scale, mm_tn(ds, qs[h]) * scale]

    def back_heads(i):
        a = 3 * (i - 1)
        natural = dqk(a) + dqk(a + 1) + dqk(a + 2) + [dv(a)]
        back(i, jnp.concatenate(natural, axis=1), jnp.concatenate([dv(a + 1), dv(a + 2)], axis=1))
        back_start(i)

    back_heads(1)
    own = mm(ogt_ref[core], zo)
    d1.wait_recv()
    d2s[...] = (own + d1r[...].astype(F32)).astype(BF).reshape(NY, 32, HD)

    def d2(k, slot):
        peer = lax.rem(y + k, NY)
        return pltpu.make_async_remote_copy(
            src_ref=d2s.at[peer], dst_ref=d2r.at[peer if slot else y], send_sem=d2_ssem.at[peer],
            recv_sem=d2_rsem.at[peer if slot else y],
            device_id=(g, col_of(zl, peer, core)), device_id_type=MESH,
        )

    def d2_start(k, c):
        d2(k, False).start()
        return c

    lax.fori_loop(1, NY, d2_start, 0)
    d2r[y] = d2s[y]
    back_heads(2)

    def chunk_home(i):
        grp_wait_recv(rs[i], rr[i], r_ssem.at[i], r_rsem.at[i])
        chunk = rr[i][...].reshape(PROWS, rr[i].shape[2])
        return mm(home_nat, chunk), chunk

    def d2_wait(k, c):
        d2(k, True).wait_recv()
        return c

    lax.fori_loop(1, NY, d2_wait, 0)
    total = d2r[0].astype(F32)
    for yy in range(1, NY):
        total = total + d2r[yy].astype(F32)
    for xx in range(NX):
        part = total[:, 192 * xx : 192 * xx + 192].astype(BF)
        d3s[xx] = jnp.concatenate([part, part[:, :64]], axis=1)

    def d3(k, slot):
        peer = lax.rem(gx + k, NX)
        return pltpu.make_async_remote_copy(
            src_ref=d3s.at[peer], dst_ref=d3r.at[peer if slot else gx], send_sem=d3_ssem.at[peer],
            recv_sem=d3_rsem.at[peer if slot else gx],
            device_id=(peer * NH + gz, col), device_id_type=MESH,
        )

    def d3_start(k, c):
        d3(k, False).start()
        return c

    lax.fori_loop(1, NX, d3_start, 0)
    d3r[gx] = d3s[gx]

    def d3_wait(k, c):
        d3(k, True).wait_recv()
        return c

    lax.fori_loop(1, NX, d3_wait, 0)
    total = d3r[0].astype(F32)
    for xx in range(1, NX):
        total = total + d3r[xx].astype(F32)
    for zz in range(NZ):
        for hh in range(NH):
            d4s[zz * NH + hh, :, :64] = total[8 * zz : 8 * zz + 8, 64 * hh : 64 * hh + 64]
            d4s[zz * NH + hh, :, 64:] = jnp.zeros((8, 64), F32)
    place = zl * NH + gz

    def d4(k, slot):
        peer, device = z_peer(k)
        return pltpu.make_async_remote_copy(
            src_ref=d4s.at[peer], dst_ref=d4r.at[peer if slot else place], send_sem=d4_ssem.at[peer],
            recv_sem=d4_rsem.at[peer if slot else place], device_id=device, device_id_type=MESH,
        )

    def d4_start(k, c):
        d4(k, False).start()
        return c

    lax.fori_loop(1, NG, d4_start, 0)
    d4r[place] = d4s[place]

    n_part, chunk = chunk_home(0)
    n_home = jnp.concatenate(
        [n_part[:, : 3 * DH], fold_out(home_fold, chunk, 1), n_part[:, 3 * DH :]], axis=1
    )
    z = (n_home * gate).astype(BF)
    pg_ref[:, :HD] = (branch * n_home).astype(BF)
    bo_ref[...] = mm(z, w_ref[...]).astype(BF)

    for i in (1, 2):
        a = 3 * (i - 1)
        part, chunk = chunk_home(i)
        part = part.astype(BF)
        for h in range(3):
            lo = 2 * HD + (a + h) * DH
            pg_ref[:, lo : lo + DH] = part[:, head(2 * h)]
            pg_ref[:, lo + HD : lo + HD + DH] = part[:, head(2 * h + 1)]
        lo = HD + a * DH
        pg_ref[:, lo : lo + DH] = part[:, head(6)]
        pg_ref[:, lo + DH : lo + 3 * DH] = fold_out(home_fold, chunk, 2).astype(BF)

    def d4_wait(k, c):
        d4(k, True).wait_recv()
        return c

    lax.fori_loop(1, NG, d4_wait, 0)
    total = d4r[0]
    for o in range(1, NG):
        total = total + d4r[o]
    dw_ref[...] = total[:, :64]

    grp_wait_send(ts, tr, t_ssem, t_rsem)
    for i in range(4):
        grp_wait_send(cs[i], cr[i], c_ssem.at[i], c_rsem.at[i])
    for i in range(3):
        grp_wait_send(rs[i], rr[i], r_ssem.at[i], r_rsem.at[i])
    d1.wait_send()

    def d2_sent(k, c):
        d2(k, False).wait_send()
        return c

    lax.fori_loop(1, NY, d2_sent, 0)

    def d3_sent(k, c):
        d3(k, False).wait_send()
        return c

    lax.fori_loop(1, NX, d3_sent, 0)

    def d4_sent(k, c):
        d4(k, False).wait_send()
        return c

    lax.fori_loop(1, NG, d4_sent, 0)


def per_device(projected, out_grad, w_out, owners, slots, lengths):
    dma = pltpu.SemaphoreType.DMA
    vmem = pl.BlockSpec(memory_space=pltpu.VMEM)
    hbm = pl.BlockSpec(memory_space=pltpu.HBM)
    smem = pl.BlockSpec(memory_space=pltpu.SMEM)
    bo, pg, dw = pl.pallas_call(
        kernel,
        out_shape=(
            jax.ShapeDtypeStruct((ROWS, 512), BF),
            jax.ShapeDtypeStruct((ROWS, 4 * HD), BF),
            jax.ShapeDtypeStruct((8, 64), F32),
        ),
        in_specs=[smem, smem, smem, hbm, hbm, hbm],
        out_specs=(vmem, vmem, vmem),
        scratch_shapes=[
            pltpu.VMEM((ROWS, 4 * HD), BF),
            pltpu.VMEM((ROWS, 512), BF),
            pltpu.VMEM((HD, 512), BF),
            dma((4,)),
            *[pltpu.VMEM((NG, PR, w), BF) for w in (768, 768, 384, 768) * 2 + (640, 896, 896) * 2],
            pltpu.VMEM((NG, 1, DH), F32),
            pltpu.VMEM((NG, 1, DH), F32),
            pltpu.VMEM((HEADS, PROWS, PROWS), BF),
            pltpu.VMEM((HEADS, PROWS, PROWS), F32),
            pltpu.VMEM((NC, 256, PROWS), BF),
            pltpu.VMEM((256, HD), BF),
            pltpu.VMEM((256, HD), BF),
            pltpu.VMEM((NY, 32, HD), BF),
            pltpu.VMEM((NY, 32, HD), BF),
            pltpu.VMEM((NX, 32, 256), BF),
            pltpu.VMEM((NX, 32, 256), BF),
            pltpu.VMEM((NG, 8, DH), F32),
            pltpu.VMEM((NG, 8, DH), F32),
            dma((4, NG)), dma((4, NG)), dma((3, NG)), dma((3, NG)), dma((NG,)), dma((NG,)),
            dma, dma, dma((NY,)), dma((NY,)), dma((NX,)), dma((NX,)), dma((NG,)), dma((NG,)),
        ],
        compiler_params=pltpu.CompilerParams(
            collective_id=0, has_side_effects=True, vmem_limit_bytes=63 * 1024 * 1024
        ),
    )(owners, slots, lengths, projected[0], out_grad[0], w_out)
    return (bo[None], pg[None], dw.T)


def solution(mesh):
    return jax.shard_map(
        per_device,
        mesh=mesh,
        in_specs=(
            P("col", "grp", None),
            P("col", "grp", None),
            P(),
            P("col", "grp"),
            P("col", "grp"),
            P("col", "grp"),
        ),
        out_specs=(P("col", "grp", None), P("col", "grp", None), P("grp", "col")),
        check_vma=False,
    )
```

```python
import functools
import math

import jax
import jax.numpy as jnp
from jax import lax
from jax.experimental import pallas as pl
from jax.experimental.pallas import tpu as pltpu
from jax.sharding import PartitionSpec as P

DH = 128
HEADS = 6
HD = 768
BR = 12
PR = 16
NG = 12
NX, NH = 4, 3
NZ, NY, NC = 4, 8, 2
ROWS = BR * NG
PROWS = PR * NG
MESH = pl.DeviceIdType.MESH
BF = jnp.bfloat16
F32 = jnp.float32


def mm(a, b):
    return lax.dot_general(a, b, (((1,), (0,)), ((), ())), preferred_element_type=F32)


def mm_nt(a, b):
    return lax.dot_general(a, b, (((1,), (1,)), ((), ())), preferred_element_type=F32)


def mm_tn(a, b):
    return lax.dot_general(a, b, (((0,), (0,)), ((), ())), preferred_element_type=F32)


def onehot(cond):
    return jnp.where(cond, 1.0, 0.0).astype(BF)


def iota(shape, dim):
    return lax.broadcasted_iota(jnp.int32, shape, dim)


def fold_in(mats, natural, folded):
    parts = [mm(mats[b], folded) for b in range(3)]
    count = folded.shape[1] // DH
    extra = [parts[b][:, head(m)] for m in range(count) for b in range(3)]
    wide = 3 * DH * count
    done = natural[:, :wide] + jnp.concatenate(extra, axis=1)
    if natural.shape[1] > wide:
        done = jnp.concatenate([done, natural[:, wide:]], axis=1)
    return done.astype(BF)


def fold_out(mats, chunk, count):
    total = None
    for b in range(3):
        lanes = [chunk[:, head(3 * m + b)] for m in range(count)]
        term = mm(mats[b], lanes[0] if count == 1 else jnp.concatenate(lanes, axis=1))
        total = term if total is None else total + term
    return total


def head(h):
    return slice(h * DH, (h + 1) * DH)


def kernel(
    own_s, slot_s, len_s, x_hbm, og_hbm, w_hbm,
    bo_ref, pg_ref, dw_ref, x_ref, og_ref, w_ref, in_sem,
    c0s, c1s, c2s, c3s, c0r, c1r, c2r, c3r, r0s, r1s, r2s, r0r, r1r, r2r,
    ts, tr, p_scr, f_scr, ogt_ref, d1s, d1r, d2s, d2r, d3s, d3r, d4s, d4r,
    c_ssem, c_rsem, r_ssem, r_rsem, t_ssem, t_rsem,
    d1_ssem, d1_rsem, d2_ssem, d2_rsem, d3_ssem, d3_rsem, d4_ssem, d4_rsem,
):
    g = lax.axis_index("grp")
    col = lax.axis_index("col")
    gx, gz = g // NH, lax.rem(g, NH)
    cs, cr = (c0s, c1s, c2s, c3s), (c0r, c1r, c2r, c3r)
    rs, rr = (r0s, r1s, r2s), (r0r, r1r, r2r)
    core = lax.rem(col, NC)
    y = lax.rem(col // NC, NY)
    zl = col // (NC * NY)

    def col_of(z_, y_, c_):
        return (z_ * NY + y_) * NC + c_

    other = col_of(zl, y, 1 - core)

    half = 2 * HD
    loads = [
        pltpu.make_async_copy(x_hbm.at[:, half:], x_ref.at[:, half:], in_sem.at[0]),
        pltpu.make_async_copy(x_hbm.at[:, :half], x_ref.at[:, :half], in_sem.at[1]),
        pltpu.make_async_copy(og_hbm, og_ref, in_sem.at[2]),
        pltpu.make_async_copy(w_hbm, w_ref, in_sem.at[3]),
    ]

    barrier = pltpu.get_barrier_semaphore()

    def greet(k, c):
        pl.semaphore_signal(
            barrier, inc=1, device_id=(lax.rem(g + k, NG), col), device_id_type=MESH
        )
        return c

    lax.fori_loop(1, NG, greet, 0)
    pl.semaphore_signal(barrier, inc=1, device_id=(g, other), device_id_type=MESH)

    def greet_y(k, c):
        pl.semaphore_signal(
            barrier, inc=1, device_id=(g, col_of(zl, lax.rem(y + k, NY), core)), device_id_type=MESH
        )
        return c

    lax.fori_loop(1, NY, greet_y, 0)

    def z_peer(k):
        place = lax.rem(zl * NH + gz + k, NG)
        return place, (gx * NH + lax.rem(place, NH), col_of(place // NH, y, core))

    def greet_z(k, c):
        pl.semaphore_signal(barrier, inc=1, device_id=z_peer(k)[1], device_id_type=MESH)
        return c

    lax.fori_loop(1, NG, greet_z, 0)
    for load in loads:
        load.start()

    def grp_copy(src, dst, ssem, rsem, k):
        peer = lax.rem(g + k, NG)
        return pltpu.make_async_remote_copy(
            src_ref=src.at[peer], dst_ref=dst.at[g], send_sem=ssem.at[peer], recv_sem=rsem.at[g],
            device_id=(peer, col), device_id_type=MESH,
        )

    def grp_start(src, dst, ssem, rsem):
        def body(k, c):
            grp_copy(src, dst, ssem, rsem, k).start()
            return c

        lax.fori_loop(1, NG, body, 0)

    def grp_wait_recv(src, dst, ssem, rsem):
        def body(k, c):
            peer = lax.rem(g + k, NG)
            pltpu.make_async_remote_copy(
                src_ref=src.at[peer], dst_ref=dst.at[peer], send_sem=ssem.at[peer],
                recv_sem=rsem.at[peer], device_id=(peer, col), device_id_type=MESH,
            ).wait_recv()
            return c

        lax.fori_loop(1, NG, body, 0)

    def grp_wait_send(src, dst, ssem, rsem):
        def body(k, c):
            grp_copy(src, dst, ssem, rsem, k).wait_send()
            return c

        lax.fori_loop(1, NG, body, 0)

    lane = iota((8, ROWS), 1)
    own_c = jnp.zeros((8, ROWS), jnp.int32)
    in_c = lane
    for j in range(NG):
        own_c = jnp.where(lane >= BR * j, own_s[0, j], own_c)
        in_c = jnp.where(lane >= BR * j, lane - BR * j, in_c)
    own_c, in_c = own_c[:1], in_c[:1]
    rows = iota((PROWS, ROWS), 0)
    same = (rows >> 4) == own_c
    in_r = rows & 15
    send_nat = onehot(same & (in_r == in_c))
    send_fold = [onehot(same & (in_r - BR + 4 * b == in_c) & (in_r >= BR)) for b in range(3)]

    def put(i, chunk):
        cs[i][...] = chunk.reshape(NG, PR, chunk.shape[1])
        cr[i][g] = cs[i][g]

    def send(i):
        grp_start(cs[i], cr[i], c_ssem.at[i], c_rsem.at[i])

    loads[0].wait()
    q = x_ref[:, 2 * HD : 3 * HD]
    put(0, fold_in(send_fold, mm(send_nat, q), x_ref[:, 3 * HD : 3 * HD + 2 * DH]))
    for o in range(NG):
        tile = jnp.zeros((1, DH), jnp.int32)
        for j in range(NG):
            tile = jnp.where(jnp.full((1, DH), own_s[0, j]) == o, slot_s[0, j], tile)
        ts[o] = tile.astype(F32)
    tr[g] = ts[g]

    pl.semaphore_wait(barrier, NG - 1 + 1 + NY - 1 + NG - 1)

    grp_start(ts, tr, t_ssem, t_rsem)
    send(0)
    loads[1].wait()
    nat = jnp.concatenate([x_ref[:, 3 * HD + 2 * DH : 4 * HD], x_ref[:, HD : HD + 2 * DH]], axis=1)
    put(1, fold_in(send_fold, mm(send_nat, nat), x_ref[:, HD + 2 * DH : HD + 4 * DH]))
    send(1)
    nat = jnp.concatenate([x_ref[:, HD + 4 * DH : half], x_ref[:, :DH]], axis=1)
    put(2, fold_in(send_fold, mm(send_nat, nat), x_ref[:, DH : 2 * DH]))
    send(2)
    loads[2].wait()
    nat = jnp.concatenate([x_ref[:, 2 * DH : HD], og_ref[:, : 2 * DH]], axis=1)
    put(3, fold_in(send_fold, mm(send_nat, nat), og_ref[:, 2 * DH :]))
    send(3)
    loads[3].wait()
    branch = mm_nt(og_ref[...], w_ref[...]).astype(BF).astype(F32)
    gate = x_ref[:, :HD].astype(F32)

    rows = iota((PROWS, PROWS), 0)
    cols = iota((PROWS, PROWS), 1)
    same = (rows >> 4) == (cols >> 4)
    rr_, cc_ = rows & 15, cols & 15
    unfold = [onehot(same & (cc_ >= BR) & (rr_ == cc_ - BR + 4 * b)) for b in range(3)]
    infold = [onehot(same & (rr_ >= BR) & (cc_ == rr_ - BR + 4 * b)) for b in range(3)]

    rows = iota((ROWS, PROWS), 0)
    cols = iota((ROWS, PROWS), 1)
    own_r = jnp.zeros((ROWS, PROWS), jnp.int32)
    in_b = rows
    for j in range(NG):
        own_r = jnp.where(rows >= BR * j, own_s[0, j], own_r)
        in_b = jnp.where(rows >= BR * j, rows - BR * j, in_b)
    same = own_r == (cols >> 4)
    cc_ = cols & 15
    home_nat = onehot(same & (cc_ == in_b))
    home_fold = [onehot(same & (cc_ >= BR) & (cc_ - BR + 4 * b == in_b)) for b in range(3)]

    grp_wait_recv(ts, tr, t_ssem, t_rsem)
    slot_r = jnp.concatenate([jnp.broadcast_to(tr[d], (PR, DH)) for d in range(NG)], axis=0)
    lane = iota((8, PROWS), 1)
    slot_c = jnp.zeros((8, PROWS), F32)
    for d in range(NG):
        slot_c = jnp.where((lane >> 4) == d, jnp.broadcast_to(tr[d][:, :1], (8, PROWS)), slot_c)
    first = jnp.int32(0)
    length = jnp.int32(1)
    first_r, len_r = jnp.zeros((PROWS, DH), F32), jnp.ones((PROWS, DH), F32)
    first_c = jnp.zeros((8, PROWS), F32)
    for s in range(NG):
        start = len_s[0, s]
        opened = start > 0
        first = jnp.where(opened, s, first)
        length = jnp.where(opened, start, length)
        first_f, length_f = first.astype(F32), length.astype(F32)
        first_r = jnp.where(slot_r == float(s), first_f, first_r)
        len_r = jnp.where(slot_r == float(s), length_f, len_r)
        first_c = jnp.where(slot_c == float(s), first_f, first_c)
    sub = iota((PROWS, DH), 0) & 15
    pos_r = (slot_r - first_r) * BR + sub.astype(F32)
    valid_r = (pos_r < len_r) & (sub < BR)
    pos_c = (slot_c - first_c) * BR + (lane & 15).astype(F32)
    pos_c = jnp.where((lane & 15) < BR, pos_c, 1e9)
    inv_r = jnp.where(valid_r, 1.0 / len_r, 0.0)
    valid = jnp.where(valid_r, 1.0, 0.0)[:, :1]
    weight = jnp.where(
        (first_r[:, :1] == first_c[:1]) & (pos_c[:1] <= pos_r[:, :1]), inv_r[:, :1], 0.0
    )

    scale = 1.0 / math.sqrt(DH)

    def chunk_in(i):
        grp_wait_recv(cs[i], cr[i], c_ssem.at[i], c_rsem.at[i])
        return cr[i][...].reshape(PROWS, cr[i].shape[2])

    c0 = chunk_in(0)
    k01 = fold_out(unfold, c0, 2).astype(BF)
    qs = [c0[:, head(h)] for h in range(HEADS)]

    def scores(h, kh):
        s = mm_nt(qs[h], kh) * scale
        sig = jax.nn.sigmoid(s)
        p_scr[h] = (s * sig * weight).astype(BF)
        f_scr[h] = sig * (1.0 + s * (1.0 - sig)) * weight

    scores(0, k01[:, :DH])
    scores(1, k01[:, DH:])
    c1 = chunk_in(1)
    ks = [k01[:, :DH], k01[:, DH:]] + [c1[:, head(h)] for h in range(4)]
    for h in range(2, HEADS):
        scores(h, ks[h])
    v23 = fold_out(unfold, c1, 2).astype(BF)
    vs = [c1[:, head(4)], c1[:, head(5)], v23[:, :DH], v23[:, DH:]]
    attended = [mm(p_scr[h], vs[h]) for h in range(4)]
    c2 = chunk_in(2)
    gate1 = fold_out(unfold, c2, 1)
    vs += [c2[:, head(0)], c2[:, head(1)]]
    attended += [mm(p_scr[h], vs[h]) for h in range(4, HEADS)]
    att = jnp.concatenate(attended, axis=1)
    centre = jnp.mean(att, axis=1, keepdims=True)
    att = att - centre
    rstd = lax.rsqrt(jnp.mean(att * att, axis=1, keepdims=True) + 1e-05)
    normed = att * rstd

    def back(i, natural, folded):
        rs[i][...] = fold_in(infold, natural, folded.astype(BF)).reshape(NG, PR, natural.shape[1])
        rr[i][g] = rs[i][g]

    def back_start(i):
        grp_start(rs[i], rr[i], r_ssem.at[i], r_rsem.at[i])

    back(0, normed[:, : 3 * DH], normed[:, head(3)])

    back_start(0)

    c3 = chunk_in(3)
    gate_o = jnp.concatenate(
        [c2[:, head(2)].astype(F32), gate1, c3[:, : 4 * DH].astype(F32)], axis=1
    )
    og_o = jnp.concatenate([c3[:, 4 * DH :], fold_out(unfold, c3, 2).astype(BF)], axis=1)

    ogt = jnp.transpose(og_o.astype(F32))
    for cc in range(NC):
        ogt_ref[cc] = jnp.concatenate(
            [
                ogt[((zz * NY + yy) * NC + cc) * 8 : ((zz * NY + yy) * NC + cc) * 8 + 8]
                for yy in range(NY)
                for zz in range(NZ)
            ],
            axis=0,
        ).astype(BF)

    zo = (normed * gate_o).astype(BF)
    d1s[...] = mm(ogt_ref[1 - core], zo).astype(BF)
    d1 = pltpu.make_async_remote_copy(
        src_ref=d1s, dst_ref=d1r, send_sem=d1_ssem, recv_sem=d1_rsem,
        device_id=(g, other), device_id_type=MESH,
    )
    d1.start()

    gr = mm_nt(og_o, w_ref[...]).astype(BF).astype(F32) * gate_o
    datt = rstd * (
        gr - jnp.mean(gr, axis=1, keepdims=True)
        - normed * jnp.mean(gr * normed, axis=1, keepdims=True)
    )
    datt = jnp.where(valid > 0.5, datt, 0.0).astype(BF)

    def dv(h):
        return mm_tn(p_scr[h], datt[:, head(h)])

    def dqk(h):
        ds = (mm_nt(datt[:, head(h)], vs[h]) * f_scr[h]).astype(BF)
        return [mm(ds, ks[h]) * scale, mm_tn(ds, qs[h]) * scale]

    natural = [normed[:, 4 * DH :]] + dqk(0) + dqk(1) + dqk(2) + [dv(0)]
    back(1, jnp.concatenate(natural, axis=1), jnp.concatenate([dv(1), dv(2), dv(3)], axis=1))
    back_start(1)
    own = mm(ogt_ref[core], zo)
    d1.wait_recv()
    d2s[...] = (own + d1r[...].astype(F32)).astype(BF).reshape(NY, 32, HD)

    def d2(k, slot):
        peer = lax.rem(y + k, NY)
        return pltpu.make_async_remote_copy(
            src_ref=d2s.at[peer], dst_ref=d2r.at[peer if slot else y], send_sem=d2_ssem.at[peer],
            recv_sem=d2_rsem.at[peer if slot else y],
            device_id=(g, col_of(zl, peer, core)), device_id_type=MESH,
        )

    def d2_start(k, c):
        d2(k, False).start()
        return c

    lax.fori_loop(1, NY, d2_start, 0)
    d2r[y] = d2s[y]
    back(2, jnp.concatenate(dqk(3) + dqk(4) + dqk(5), axis=1), jnp.concatenate([dv(4), dv(5)], axis=1))

    def chunk_home(i):
        grp_wait_recv(rs[i], rr[i], r_ssem.at[i], r_rsem.at[i])
        chunk = rr[i][...].reshape(PROWS, rr[i].shape[2])
        return mm(home_nat, chunk), chunk

    def d2_wait(k, c):
        d2(k, True).wait_recv()
        return c

    lax.fori_loop(1, NY, d2_wait, 0)
    total = d2r[0].astype(F32)
    for yy in range(1, NY):
        total = total + d2r[yy].astype(F32)
    for xx in range(NX):
        part = total[:, 192 * xx : 192 * xx + 192].astype(BF)
        d3s[xx] = jnp.concatenate([part, part[:, :64]], axis=1)

    def d3(k, slot):
        peer = lax.rem(gx + k, NX)
        return pltpu.make_async_remote_copy(
            src_ref=d3s.at[peer], dst_ref=d3r.at[peer if slot else gx], send_sem=d3_ssem.at[peer],
            recv_sem=d3_rsem.at[peer if slot else gx],
            device_id=(peer * NH + gz, col), device_id_type=MESH,
        )

    def d3_start(k, c):
        d3(k, False).start()
        return c

    lax.fori_loop(1, NX, d3_start, 0)
    back_start(2)
    d3r[gx] = d3s[gx]

    def d3_wait(k, c):
        d3(k, True).wait_recv()
        return c

    lax.fori_loop(1, NX, d3_wait, 0)
    total = d3r[0].astype(F32)
    for xx in range(1, NX):
        total = total + d3r[xx].astype(F32)
    for zz in range(NZ):
        for hh in range(NH):
            d4s[zz * NH + hh, :, :64] = total[8 * zz : 8 * zz + 8, 64 * hh : 64 * hh + 64]
            d4s[zz * NH + hh, :, 64:] = jnp.zeros((8, 64), F32)
    place = zl * NH + gz

    def d4(k, slot):
        peer, device = z_peer(k)
        return pltpu.make_async_remote_copy(
            src_ref=d4s.at[peer], dst_ref=d4r.at[peer if slot else place], send_sem=d4_ssem.at[peer],
            recv_sem=d4_rsem.at[peer if slot else place], device_id=device, device_id_type=MESH,
        )

    def d4_start(k, c):
        d4(k, False).start()
        return c

    lax.fori_loop(1, NG, d4_start, 0)
    d4r[place] = d4s[place]

    n_part, chunk0 = chunk_home(0)
    part, chunk = chunk_home(1)
    n_home = jnp.concatenate(
        [n_part, fold_out(home_fold, chunk0, 1), part[:, : 2 * DH]], axis=1
    )
    z = (n_home * gate).astype(BF)
    pg_ref[:, :HD] = (branch * n_home).astype(BF)
    bo_ref[...] = mm(z, w_ref[...]).astype(BF)
    part = part.astype(BF)
    for h in range(3):
        lo = 2 * HD + h * DH
        pg_ref[:, lo : lo + DH] = part[:, head(2 * h + 2)]
        pg_ref[:, lo + HD : lo + HD + DH] = part[:, head(2 * h + 3)]
    pg_ref[:, HD : HD + DH] = part[:, head(8)]
    pg_ref[:, HD + DH : HD + 4 * DH] = fold_out(home_fold, chunk, 3).astype(BF)
    part, chunk = chunk_home(2)
    part = part.astype(BF)
    for h in range(3):
        lo = 2 * HD + (h + 3) * DH
        pg_ref[:, lo : lo + DH] = part[:, head(2 * h)]
        pg_ref[:, lo + HD : lo + HD + DH] = part[:, head(2 * h + 1)]
    pg_ref[:, HD + 4 * DH : half] = fold_out(home_fold, chunk, 2).astype(BF)

    def d4_wait(k, c):
        d4(k, True).wait_recv()
        return c

    lax.fori_loop(1, NG, d4_wait, 0)
    total = d4r[0]
    for o in range(1, NG):
        total = total + d4r[o]
    dw_ref[...] = total[:, :64]

    grp_wait_send(ts, tr, t_ssem, t_rsem)
    for i in range(4):
        grp_wait_send(cs[i], cr[i], c_ssem.at[i], c_rsem.at[i])
    for i in range(3):
        grp_wait_send(rs[i], rr[i], r_ssem.at[i], r_rsem.at[i])
    d1.wait_send()

    def d2_sent(k, c):
        d2(k, False).wait_send()
        return c

    lax.fori_loop(1, NY, d2_sent, 0)

    def d3_sent(k, c):
        d3(k, False).wait_send()
        return c

    lax.fori_loop(1, NX, d3_sent, 0)

    def d4_sent(k, c):
        d4(k, False).wait_send()
        return c

    lax.fori_loop(1, NG, d4_sent, 0)


def per_device(projected, out_grad, w_out, owners, slots, lengths):
    dma = pltpu.SemaphoreType.DMA
    vmem = pl.BlockSpec(memory_space=pltpu.VMEM)
    hbm = pl.BlockSpec(memory_space=pltpu.HBM)
    smem = pl.BlockSpec(memory_space=pltpu.SMEM)
    bo, pg, dw = pl.pallas_call(
        kernel,
        out_shape=(
            jax.ShapeDtypeStruct((ROWS, 512), BF),
            jax.ShapeDtypeStruct((ROWS, 4 * HD), BF),
            jax.ShapeDtypeStruct((8, 64), F32),
        ),
        in_specs=[smem, smem, smem, hbm, hbm, hbm],
        out_specs=(vmem, vmem, vmem),
        scratch_shapes=[
            pltpu.VMEM((ROWS, 4 * HD), BF),
            pltpu.VMEM((ROWS, 512), BF),
            pltpu.VMEM((HD, 512), BF),
            dma((4,)),
            *[pltpu.VMEM((NG, PR, w), BF) for w in (768, 768, 384, 768) * 2 + (384, 1152, 768) * 2],
            pltpu.VMEM((NG, 1, DH), F32),
            pltpu.VMEM((NG, 1, DH), F32),
            pltpu.VMEM((HEADS, PROWS, PROWS), BF),
            pltpu.VMEM((HEADS, PROWS, PROWS), F32),
            pltpu.VMEM((NC, 256, PROWS), BF),
            pltpu.VMEM((256, HD), BF),
            pltpu.VMEM((256, HD), BF),
            pltpu.VMEM((NY, 32, HD), BF),
            pltpu.VMEM((NY, 32, HD), BF),
            pltpu.VMEM((NX, 32, 256), BF),
            pltpu.VMEM((NX, 32, 256), BF),
            pltpu.VMEM((NG, 8, DH), F32),
            pltpu.VMEM((NG, 8, DH), F32),
            dma((4, NG)), dma((4, NG)), dma((3, NG)), dma((3, NG)), dma((NG,)), dma((NG,)),
            dma, dma, dma((NY,)), dma((NY,)), dma((NX,)), dma((NX,)), dma((NG,)), dma((NG,)),
        ],
        compiler_params=pltpu.CompilerParams(
            collective_id=0, has_side_effects=True, vmem_limit_bytes=63 * 1024 * 1024
        ),
    )(owners, slots, lengths, projected[0], out_grad[0], w_out)
    return (bo[None], pg[None], dw.T)


def solution(mesh):
    return jax.shard_map(
        per_device,
        mesh=mesh,
        in_specs=(
            P("col", "grp", None),
            P("col", "grp", None),
            P(),
            P("col", "grp"),
            P("col", "grp"),
            P("col", "grp"),
        ),
        out_specs=(P("col", "grp", None), P("col", "grp", None), P("grp", "col")),
        check_vma=False,
    )
```

```python
import functools
import math

import jax
import jax.numpy as jnp
from jax import lax
from jax.experimental import pallas as pl
from jax.experimental.pallas import tpu as pltpu
from jax.sharding import PartitionSpec as P

DH = 128
HEADS = 6
HD = 768
BR = 12
PR = 16
NG = 12
NX, NH = 4, 3
NZ, NY, NC = 4, 8, 2
ROWS = BR * NG
PROWS = PR * NG
MESH = pl.DeviceIdType.MESH
BF = jnp.bfloat16
F32 = jnp.float32


def mm(a, b):
    return lax.dot_general(a, b, (((1,), (0,)), ((), ())), preferred_element_type=F32)


def mm_nt(a, b):
    return lax.dot_general(a, b, (((1,), (1,)), ((), ())), preferred_element_type=F32)


def mm_tn(a, b):
    return lax.dot_general(a, b, (((0,), (0,)), ((), ())), preferred_element_type=F32)


def onehot(cond):
    return jnp.where(cond, 1.0, 0.0).astype(BF)


def iota(shape, dim):
    return lax.broadcasted_iota(jnp.int32, shape, dim)


def fold_in(mats, natural, folded):
    parts = [mm(mats[b], folded) for b in range(3)]
    count = folded.shape[1] // DH
    extra = [parts[b][:, head(m)] for m in range(count) for b in range(3)]
    wide = 3 * DH * count
    done = natural[:, :wide] + jnp.concatenate(extra, axis=1)
    if natural.shape[1] > wide:
        done = jnp.concatenate([done, natural[:, wide:]], axis=1)
    return done.astype(BF)


def fold_out(mats, chunk, count):
    total = None
    for b in range(3):
        lanes = [chunk[:, head(3 * m + b)] for m in range(count)]
        term = mm(mats[b], lanes[0] if count == 1 else jnp.concatenate(lanes, axis=1))
        total = term if total is None else total + term
    return total


def head(h):
    return slice(h * DH, (h + 1) * DH)


def kernel(
    own_s, slot_s, len_s, x_hbm, og_hbm, w_hbm,
    bo_ref, pg_ref, dw_ref, x_ref, og_ref, w_ref, in_sem,
    c0s, c1s, c2s, c3s, c0r, c1r, c2r, c3r, r0s, r1s, r2s, r0r, r1r, r2r,
    ts, tr, p_scr, f_scr, ogt_ref, d1s, d1r, d2s, d2r, d3s, d3r, d4s, d4r,
    c_ssem, c_rsem, r_ssem, r_rsem, t_ssem, t_rsem,
    d1_ssem, d1_rsem, d2_ssem, d2_rsem, d3_ssem, d3_rsem, d4_ssem, d4_rsem,
):
    g = lax.axis_index("grp")
    col = lax.axis_index("col")
    gx, gz = g // NH, lax.rem(g, NH)
    cs, cr = (c0s, c1s, c2s, c3s), (c0r, c1r, c2r, c3r)
    rs, rr = (r0s, r1s, r2s), (r0r, r1r, r2r)
    core = lax.rem(col, NC)
    y = lax.rem(col // NC, NY)
    zl = col // (NC * NY)

    def col_of(z_, y_, c_):
        return (z_ * NY + y_) * NC + c_

    other = col_of(zl, y, 1 - core)

    half = 2 * HD
    loads = [
        pltpu.make_async_copy(x_hbm.at[:, half:], x_ref.at[:, half:], in_sem.at[0]),
        pltpu.make_async_copy(x_hbm.at[:, :half], x_ref.at[:, :half], in_sem.at[1]),
        pltpu.make_async_copy(og_hbm, og_ref, in_sem.at[2]),
        pltpu.make_async_copy(w_hbm, w_ref, in_sem.at[3]),
    ]

    barrier = pltpu.get_barrier_semaphore()

    def greet(k, c):
        pl.semaphore_signal(
            barrier, inc=1, device_id=(lax.rem(g + k, NG), col), device_id_type=MESH
        )
        return c

    lax.fori_loop(1, NG, greet, 0)
    pl.semaphore_signal(barrier, inc=1, device_id=(g, other), device_id_type=MESH)

    def greet_y(k, c):
        pl.semaphore_signal(
            barrier, inc=1, device_id=(g, col_of(zl, lax.rem(y + k, NY), core)), device_id_type=MESH
        )
        return c

    lax.fori_loop(1, NY, greet_y, 0)

    def z_peer(k):
        place = lax.rem(zl * NH + gz + k, NG)
        return place, (gx * NH + lax.rem(place, NH), col_of(place // NH, y, core))

    def greet_z(k, c):
        pl.semaphore_signal(barrier, inc=1, device_id=z_peer(k)[1], device_id_type=MESH)
        return c

    lax.fori_loop(1, NG, greet_z, 0)
    for load in loads:
        load.start()

    def grp_copy(src, dst, ssem, rsem, k):
        peer = lax.rem(g + k, NG)
        return pltpu.make_async_remote_copy(
            src_ref=src.at[peer], dst_ref=dst.at[g], send_sem=ssem.at[peer], recv_sem=rsem.at[g],
            device_id=(peer, col), device_id_type=MESH,
        )

    def grp_start(src, dst, ssem, rsem):
        def body(k, c):
            grp_copy(src, dst, ssem, rsem, k).start()
            return c

        lax.fori_loop(1, NG, body, 0)

    def grp_wait_recv(src, dst, ssem, rsem):
        def body(k, c):
            peer = lax.rem(g + k, NG)
            pltpu.make_async_remote_copy(
                src_ref=src.at[peer], dst_ref=dst.at[peer], send_sem=ssem.at[peer],
                recv_sem=rsem.at[peer], device_id=(peer, col), device_id_type=MESH,
            ).wait_recv()
            return c

        lax.fori_loop(1, NG, body, 0)

    def grp_wait_send(src, dst, ssem, rsem):
        def body(k, c):
            grp_copy(src, dst, ssem, rsem, k).wait_send()
            return c

        lax.fori_loop(1, NG, body, 0)

    lane = iota((8, ROWS), 1)
    own_c = jnp.zeros((8, ROWS), jnp.int32)
    in_c = lane
    for j in range(NG):
        own_c = jnp.where(lane >= BR * j, own_s[0, j], own_c)
        in_c = jnp.where(lane >= BR * j, lane - BR * j, in_c)
    own_c, in_c = own_c[:1], in_c[:1]
    rows = iota((PROWS, ROWS), 0)
    same = (rows >> 4) == own_c
    in_r = rows & 15
    send_nat = onehot(same & (in_r == in_c))
    send_fold = [onehot(same & (in_r - BR + 4 * b == in_c) & (in_r >= BR)) for b in range(3)]

    def put(i, chunk):
        cs[i][...] = chunk.reshape(NG, PR, chunk.shape[1])
        cr[i][g] = cs[i][g]

    def send(i):
        grp_start(cs[i], cr[i], c_ssem.at[i], c_rsem.at[i])

    loads[0].wait()
    q = x_ref[:, 2 * HD : 3 * HD]
    put(0, fold_in(send_fold, mm(send_nat, q), x_ref[:, 3 * HD : 3 * HD + 2 * DH]))
    for o in range(NG):
        tile = jnp.zeros((1, DH), jnp.int32)
        for j in range(NG):
            tile = jnp.where(jnp.full((1, DH), own_s[0, j]) == o, slot_s[0, j], tile)
        ts[o] = tile.astype(F32)
    tr[g] = ts[g]

    pl.semaphore_wait(barrier, NG - 1 + 1 + NY - 1 + NG - 1)

    grp_start(ts, tr, t_ssem, t_rsem)
    send(0)
    loads[1].wait()
    nat = jnp.concatenate([x_ref[:, 3 * HD + 2 * DH : 4 * HD], x_ref[:, HD : HD + 2 * DH]], axis=1)
    put(1, fold_in(send_fold, mm(send_nat, nat), x_ref[:, HD + 2 * DH : HD + 4 * DH]))
    send(1)
    nat = jnp.concatenate([x_ref[:, HD + 4 * DH : half], x_ref[:, :DH]], axis=1)
    put(2, fold_in(send_fold, mm(send_nat, nat), x_ref[:, DH : 2 * DH]))
    send(2)
    loads[2].wait()
    nat = jnp.concatenate([x_ref[:, 2 * DH : HD], og_ref[:, : 2 * DH]], axis=1)
    put(3, fold_in(send_fold, mm(send_nat, nat), og_ref[:, 2 * DH :]))
    send(3)
    loads[3].wait()
    branch = mm_nt(og_ref[...], w_ref[...]).astype(BF).astype(F32)
    gate = x_ref[:, :HD].astype(F32)

    rows = iota((PROWS, PROWS), 0)
    cols = iota((PROWS, PROWS), 1)
    same = (rows >> 4) == (cols >> 4)
    rr_, cc_ = rows & 15, cols & 15
    unfold = [onehot(same & (cc_ >= BR) & (rr_ == cc_ - BR + 4 * b)) for b in range(3)]
    infold = [onehot(same & (rr_ >= BR) & (cc_ == rr_ - BR + 4 * b)) for b in range(3)]

    rows = iota((ROWS, PROWS), 0)
    cols = iota((ROWS, PROWS), 1)
    own_r = jnp.zeros((ROWS, PROWS), jnp.int32)
    in_b = rows
    for j in range(NG):
        own_r = jnp.where(rows >= BR * j, own_s[0, j], own_r)
        in_b = jnp.where(rows >= BR * j, rows - BR * j, in_b)
    same = own_r == (cols >> 4)
    cc_ = cols & 15
    home_nat = onehot(same & (cc_ == in_b))
    home_fold = [onehot(same & (cc_ >= BR) & (cc_ - BR + 4 * b == in_b)) for b in range(3)]

    grp_wait_recv(ts, tr, t_ssem, t_rsem)
    slot_r = jnp.concatenate([jnp.broadcast_to(tr[d], (PR, DH)) for d in range(NG)], axis=0)
    lane = iota((8, PROWS), 1)
    slot_c = jnp.zeros((8, PROWS), F32)
    for d in range(NG):
        slot_c = jnp.where((lane >> 4) == d, jnp.broadcast_to(tr[d][:, :1], (8, PROWS)), slot_c)
    first = jnp.int32(0)
    length = jnp.int32(1)
    first_r, len_r = jnp.zeros((PROWS, DH), F32), jnp.ones((PROWS, DH), F32)
    first_c = jnp.zeros((8, PROWS), F32)
    for s in range(NG):
        start = len_s[0, s]
        opened = start > 0
        first = jnp.where(opened, s, first)
        length = jnp.where(opened, start, length)
        first_f, length_f = first.astype(F32), length.astype(F32)
        first_r = jnp.where(slot_r == float(s), first_f, first_r)
        len_r = jnp.where(slot_r == float(s), length_f, len_r)
        first_c = jnp.where(slot_c == float(s), first_f, first_c)
    sub = iota((PROWS, DH), 0) & 15
    pos_r = (slot_r - first_r) * BR + sub.astype(F32)
    valid_r = (pos_r < len_r) & (sub < BR)
    pos_c = (slot_c - first_c) * BR + (lane & 15).astype(F32)
    pos_c = jnp.where((lane & 15) < BR, pos_c, 1e9)
    inv_r = jnp.where(valid_r, 1.0 / len_r, 0.0)
    valid = jnp.where(valid_r, 1.0, 0.0)[:, :1]
    weight = jnp.where(
        (first_r[:, :1] == first_c[:1]) & (pos_c[:1] <= pos_r[:, :1]), inv_r[:, :1], 0.0
    )

    scale = 1.0 / math.sqrt(DH)

    def chunk_in(i):
        grp_wait_recv(cs[i], cr[i], c_ssem.at[i], c_rsem.at[i])
        return cr[i][...].reshape(PROWS, cr[i].shape[2])

    c0 = chunk_in(0)
    k01 = fold_out(unfold, c0, 2).astype(BF)
    qs = [c0[:, head(h)] for h in range(HEADS)]

    def scores(h, kh):
        s = mm_nt(qs[h], kh) * scale
        sig = jax.nn.sigmoid(s)
        p_scr[h] = (s * sig * weight).astype(BF)
        f_scr[h] = sig * (1.0 + s * (1.0 - sig)) * weight

    scores(0, k01[:, :DH])
    scores(1, k01[:, DH:])
    c1 = chunk_in(1)
    ks = [k01[:, :DH], k01[:, DH:]] + [c1[:, head(h)] for h in range(4)]
    for h in range(2, HEADS):
        scores(h, ks[h])
    v23 = fold_out(unfold, c1, 2).astype(BF)
    vs = [c1[:, head(4)], c1[:, head(5)], v23[:, :DH], v23[:, DH:]]
    attended = [mm(p_scr[h], vs[h]) for h in range(4)]
    c2 = chunk_in(2)
    gate1 = fold_out(unfold, c2, 1)
    vs += [c2[:, head(0)], c2[:, head(1)]]
    attended += [mm(p_scr[h], vs[h]) for h in range(4, HEADS)]
    att = jnp.concatenate(attended, axis=1)
    centre = jnp.mean(att, axis=1, keepdims=True)
    att = att - centre
    rstd = lax.rsqrt(jnp.mean(att * att, axis=1, keepdims=True) + 1e-05)
    normed = att * rstd

    def back(i, natural, folded):
        rs[i][...] = fold_in(infold, natural, folded.astype(BF)).reshape(NG, PR, natural.shape[1])
        rr[i][g] = rs[i][g]

    def back_start(i):
        grp_start(rs[i], rr[i], r_ssem.at[i], r_rsem.at[i])

    back(0, normed[:, : 3 * DH], normed[:, head(3)])

    back_start(0)

    c3 = chunk_in(3)
    gate_o = jnp.concatenate(
        [c2[:, head(2)].astype(F32), gate1, c3[:, : 4 * DH].astype(F32)], axis=1
    )
    og_o = jnp.concatenate([c3[:, 4 * DH :], fold_out(unfold, c3, 2).astype(BF)], axis=1)

    gr = mm_nt(og_o, w_ref[...]).astype(BF).astype(F32) * gate_o
    datt = rstd * (
        gr - jnp.mean(gr, axis=1, keepdims=True)
        - normed * jnp.mean(gr * normed, axis=1, keepdims=True)
    )
    datt = jnp.where(valid > 0.5, datt, 0.0).astype(BF)

    def dv(h):
        return mm_tn(p_scr[h], datt[:, head(h)])

    def dqk(h):
        ds = (mm_nt(datt[:, head(h)], vs[h]) * f_scr[h]).astype(BF)
        return [mm(ds, ks[h]) * scale, mm_tn(ds, qs[h]) * scale]

    natural = [normed[:, 4 * DH :]] + dqk(0) + dqk(1) + dqk(2) + [dv(0)]
    back(1, jnp.concatenate(natural, axis=1), jnp.concatenate([dv(1), dv(2), dv(3)], axis=1))
    back_start(1)

    ogt = jnp.transpose(og_o.astype(F32))
    for cc in range(NC):
        ogt_ref[cc] = jnp.concatenate(
            [
                ogt[((zz * NY + yy) * NC + cc) * 8 : ((zz * NY + yy) * NC + cc) * 8 + 8]
                for yy in range(NY)
                for zz in range(NZ)
            ],
            axis=0,
        ).astype(BF)

    zo = (normed * gate_o).astype(BF)
    d1s[...] = mm(ogt_ref[1 - core], zo).astype(BF)
    d1 = pltpu.make_async_remote_copy(
        src_ref=d1s, dst_ref=d1r, send_sem=d1_ssem, recv_sem=d1_rsem,
        device_id=(g, other), device_id_type=MESH,
    )
    d1.start()
    own = mm(ogt_ref[core], zo)
    d1.wait_recv()
    d2s[...] = (own + d1r[...].astype(F32)).astype(BF).reshape(NY, 32, HD)

    def d2(k, slot):
        peer = lax.rem(y + k, NY)
        return pltpu.make_async_remote_copy(
            src_ref=d2s.at[peer], dst_ref=d2r.at[peer if slot else y], send_sem=d2_ssem.at[peer],
            recv_sem=d2_rsem.at[peer if slot else y],
            device_id=(g, col_of(zl, peer, core)), device_id_type=MESH,
        )

    def d2_start(k, c):
        d2(k, False).start()
        return c

    lax.fori_loop(1, NY, d2_start, 0)
    d2r[y] = d2s[y]
    back(2, jnp.concatenate(dqk(3) + dqk(4) + dqk(5), axis=1), jnp.concatenate([dv(4), dv(5)], axis=1))

    def chunk_home(i):
        grp_wait_recv(rs[i], rr[i], r_ssem.at[i], r_rsem.at[i])
        chunk = rr[i][...].reshape(PROWS, rr[i].shape[2])
        return mm(home_nat, chunk), chunk

    def d2_wait(k, c):
        d2(k, True).wait_recv()
        return c

    lax.fori_loop(1, NY, d2_wait, 0)
    total = d2r[0].astype(F32)
    for yy in range(1, NY):
        total = total + d2r[yy].astype(F32)
    for xx in range(NX):
        part = total[:, 192 * xx : 192 * xx + 192].astype(BF)
        d3s[xx] = jnp.concatenate([part, part[:, :64]], axis=1)

    def d3(k, slot):
        peer = lax.rem(gx + k, NX)
        return pltpu.make_async_remote_copy(
            src_ref=d3s.at[peer], dst_ref=d3r.at[peer if slot else gx], send_sem=d3_ssem.at[peer],
            recv_sem=d3_rsem.at[peer if slot else gx],
            device_id=(peer * NH + gz, col), device_id_type=MESH,
        )

    def d3_start(k, c):
        d3(k, False).start()
        return c

    lax.fori_loop(1, NX, d3_start, 0)
    back_start(2)
    d3r[gx] = d3s[gx]

    def d3_wait(k, c):
        d3(k, True).wait_recv()
        return c

    lax.fori_loop(1, NX, d3_wait, 0)
    total = d3r[0].astype(F32)
    for xx in range(1, NX):
        total = total + d3r[xx].astype(F32)
    for zz in range(NZ):
        for hh in range(NH):
            d4s[zz * NH + hh, :, :64] = total[8 * zz : 8 * zz + 8, 64 * hh : 64 * hh + 64]
            d4s[zz * NH + hh, :, 64:] = jnp.zeros((8, 64), F32)
    place = zl * NH + gz

    def d4(k, slot):
        peer, device = z_peer(k)
        return pltpu.make_async_remote_copy(
            src_ref=d4s.at[peer], dst_ref=d4r.at[peer if slot else place], send_sem=d4_ssem.at[peer],
            recv_sem=d4_rsem.at[peer if slot else place], device_id=device, device_id_type=MESH,
        )

    def d4_start(k, c):
        d4(k, False).start()
        return c

    lax.fori_loop(1, NG, d4_start, 0)
    d4r[place] = d4s[place]

    n_part, chunk0 = chunk_home(0)
    part, chunk = chunk_home(1)
    n_home = jnp.concatenate(
        [n_part, fold_out(home_fold, chunk0, 1), part[:, : 2 * DH]], axis=1
    )
    z = (n_home * gate).astype(BF)
    pg_ref[:, :HD] = (branch * n_home).astype(BF)
    bo_ref[...] = mm(z, w_ref[...]).astype(BF)
    part = part.astype(BF)
    for h in range(3):
        lo = 2 * HD + h * DH
        pg_ref[:, lo : lo + DH] = part[:, head(2 * h + 2)]
        pg_ref[:, lo + HD : lo + HD + DH] = part[:, head(2 * h + 3)]
    pg_ref[:, HD : HD + DH] = part[:, head(8)]
    pg_ref[:, HD + DH : HD + 4 * DH] = fold_out(home_fold, chunk, 3).astype(BF)
    part, chunk = chunk_home(2)
    part = part.astype(BF)
    for h in range(3):
        lo = 2 * HD + (h + 3) * DH
        pg_ref[:, lo : lo + DH] = part[:, head(2 * h)]
        pg_ref[:, lo + HD : lo + HD + DH] = part[:, head(2 * h + 1)]
    pg_ref[:, HD + 4 * DH : half] = fold_out(home_fold, chunk, 2).astype(BF)

    def d4_wait(k, c):
        d4(k, True).wait_recv()
        return c

    lax.fori_loop(1, NG, d4_wait, 0)
    total = d4r[0]
    for o in range(1, NG):
        total = total + d4r[o]
    dw_ref[...] = total[:, :64]

    grp_wait_send(ts, tr, t_ssem, t_rsem)
    for i in range(4):
        grp_wait_send(cs[i], cr[i], c_ssem.at[i], c_rsem.at[i])
    for i in range(3):
        grp_wait_send(rs[i], rr[i], r_ssem.at[i], r_rsem.at[i])
    d1.wait_send()

    def d2_sent(k, c):
        d2(k, False).wait_send()
        return c

    lax.fori_loop(1, NY, d2_sent, 0)

    def d3_sent(k, c):
        d3(k, False).wait_send()
        return c

    lax.fori_loop(1, NX, d3_sent, 0)

    def d4_sent(k, c):
        d4(k, False).wait_send()
        return c

    lax.fori_loop(1, NG, d4_sent, 0)


def per_device(projected, out_grad, w_out, owners, slots, lengths):
    dma = pltpu.SemaphoreType.DMA
    vmem = pl.BlockSpec(memory_space=pltpu.VMEM)
    hbm = pl.BlockSpec(memory_space=pltpu.HBM)
    smem = pl.BlockSpec(memory_space=pltpu.SMEM)
    bo, pg, dw = pl.pallas_call(
        kernel,
        out_shape=(
            jax.ShapeDtypeStruct((ROWS, 512), BF),
            jax.ShapeDtypeStruct((ROWS, 4 * HD), BF),
            jax.ShapeDtypeStruct((8, 64), F32),
        ),
        in_specs=[smem, smem, smem, hbm, hbm, hbm],
        out_specs=(vmem, vmem, vmem),
        scratch_shapes=[
            pltpu.VMEM((ROWS, 4 * HD), BF),
            pltpu.VMEM((ROWS, 512), BF),
            pltpu.VMEM((HD, 512), BF),
            dma((4,)),
            *[pltpu.VMEM((NG, PR, w), BF) for w in (768, 768, 384, 768) * 2 + (384, 1152, 768) * 2],
            pltpu.VMEM((NG, 1, DH), F32),
            pltpu.VMEM((NG, 1, DH), F32),
            pltpu.VMEM((HEADS, PROWS, PROWS), BF),
            pltpu.VMEM((HEADS, PROWS, PROWS), F32),
            pltpu.VMEM((NC, 256, PROWS), BF),
            pltpu.VMEM((256, HD), BF),
            pltpu.VMEM((256, HD), BF),
            pltpu.VMEM((NY, 32, HD), BF),
            pltpu.VMEM((NY, 32, HD), BF),
            pltpu.VMEM((NX, 32, 256), BF),
            pltpu.VMEM((NX, 32, 256), BF),
            pltpu.VMEM((NG, 8, DH), F32),
            pltpu.VMEM((NG, 8, DH), F32),
            dma((4, NG)), dma((4, NG)), dma((3, NG)), dma((3, NG)), dma((NG,)), dma((NG,)),
            dma, dma, dma((NY,)), dma((NY,)), dma((NX,)), dma((NX,)), dma((NG,)), dma((NG,)),
        ],
        compiler_params=pltpu.CompilerParams(
            collective_id=0, has_side_effects=True, vmem_limit_bytes=63 * 1024 * 1024
        ),
    )(owners, slots, lengths, projected[0], out_grad[0], w_out)
    return (bo[None], pg[None], dw.T)


def solution(mesh):
    return jax.shard_map(
        per_device,
        mesh=mesh,
        in_specs=(
            P("col", "grp", None),
            P("col", "grp", None),
            P(),
            P("col", "grp"),
            P("col", "grp"),
            P("col", "grp"),
        ),
        out_specs=(P("col", "grp", None), P("col", "grp", None), P("grp", "col")),
        check_vma=False,
    )
```
